32 devices in a mesh: tm: 8 (over y, x, core), group: 4 (over z).
Axes of the slice: x: 2, y: 2, z: 4, core: 2. Of those that a mesh axis runs over, the one named last changes fastest.
Arguments:
- clips: bfloat16 [4, 64, 128, 512], P('group', 'tm'), may hold values from -6 to 6
- lengths: int32 [4, 8], P('group'), may hold values from 1 to 16, 64 in all within a row
- w_time: bfloat16 [3, 512, 512], P(None, 'tm'), may hold values from -0.15625 to 0.15625
- w_down: bfloat16 [3, 512, 512], P(None, 'tm'), may hold values from -0.15625 to 0.15625
- cotangent: bfloat16 [4, 32, 128, 512], P('group', 'tm'), may hold values from -6 to 6
Outputs:
- reduced: bfloat16 [4, 32, 128, 512], P('group', 'tm')
- grad_clips: bfloat16 [4, 64, 128, 512], P('group', 'tm')
- grad_time: float32 [3, 512, 512], P(None, 'tm')
- grad_down: float32 [3, 512, 512], P(None, 'tm')
The draws below stay inside these ranges and needn't reach their ends.
All inputs are finite; a program needn't handle non-finite values.
Results may differ from the reference program's by a relative error of at most 0.0052.
Values may be sent and summed in bfloat16 or wider, within the bound.
No kernel may reach another device: no remote copies, remote signals or barrier semaphores. Data moves between devices by JAX's collectives and lax.ppermute only.
A program may use at most 64 MiB of HBM per device.

```python
import math
import jax
import jax.numpy as jnp
import numpy as np
from jax import lax

C = 512
S = 128
FD = 8
NC = 8
KT = 3
FR = 64
HALF = 32
GROUPS = 4
N_TM = 8


def raised(values, own_key, source, target, blocks, factor):
    def block_of(axis_at):
        return (jnp.arange(values.shape[axis_at]) // (values.shape[axis_at] // blocks)).reshape((-1,) + (1,) * (values.ndim - 1 - axis_at))

    first = jax.random.permutation(own_key, blocks)[block_of(target)]
    other_side = (block_of(target) + blocks // 2) % blocks
    return jnp.where((block_of(source) == first) | (block_of(source) == other_side), factor * values, values)


def shard_levels(rng, dims, pieces, least, high):
    level = 1.0
    for axis_at, blocks in pieces:
        heights = jax.random.uniform(jax.random.fold_in(jax.random.fold_in(rng, 6), axis_at), (blocks,), jnp.float32, least / len(pieces), high / len(pieces))
        level = level * jnp.repeat(jnp.exp(heights), dims[axis_at] // blocks).reshape((-1,) + (1,) * (len(dims) - 1 - axis_at))
    return level


def length_profile(amount, total, limit, skew):
    portions = [(1 << 20) // math.isqrt(rank ** skew) + 1 for rank in range(2, amount + 1)]
    surplus, holding = total - limit - (amount - 1), [1] * (amount - 1)
    while surplus > 0:
        movable = [i for i in range(amount - 1) if holding[i] < limit]
        pool, budget = sum([portions[i] for i in movable]), surplus
        for i in movable:
            addition = min(limit - holding[i], max(1, budget * portions[i] // pool), surplus)
            holding[i] = holding[i] + addition
            surplus = surplus - addition
    return np.array([limit] + holding)


def ragged(own_key, count, total, bound, slope):
    if count == 2:
        one = jax.random.randint(own_key, (), max(1, total - bound), min(bound, total - 1) + 1)
        return jnp.stack([one, total - one])
    sizes = jnp.asarray(length_profile(count, total, bound, slope), jnp.int32)
    couples = (count - 1) // 2
    source_of, sink = sizes[1:1 + 2 * couples:2], sizes[2:2 + 2 * couples:2]
    room = jnp.minimum(source_of - 1, bound - sink)
    shifted = jax.random.randint(jax.random.fold_in(own_key, 1), (couples,), 0, 1 << 20) % (room + 1)
    sizes = sizes.at[1:1 + 2 * couples:2].set(source_of - shifted).at[2:2 + 2 * couples:2].set(sink + shifted)
    return sizes[jax.random.permutation(jax.random.fold_in(own_key, 2), count)]


def bell_draw(own_key, shape, scale, limit, shards=(), kind=jnp.bfloat16):
    result = jax.random.normal(own_key, shape, jnp.float32) * scale
    if len(shards) > 0:
        result = shard_levels(own_key, shape, shards, -0.22, 0.18) * result
    return jnp.clip(result, min=-limit, max=limit).astype(kind)


def bell_draw_with(rng, shape, scale, bound, pieces, heavy, held_as=jnp.bfloat16):
    entries = scale * jax.random.normal(rng, shape, jnp.float32)
    if pieces:
        entries = entries * shard_levels(rng, shape, pieces, -0.22, 0.18)
    return jnp.clip(raised(entries, jax.random.fold_in(rng, 3), *heavy), -bound, bound).astype(held_as)


def setup_inputs(seed: int = 0) -> dict:
    arg_keys = jax.random.split(jax.random.key(seed), 6)
    return {
        "clips": bell_draw_with(arg_keys[0], (GROUPS, FR, S, C), 1.0, 6.0, ((0, 4), (1, 8)), (1, 3, 8, 2.0)),
        "lengths": jax.vmap(lambda own: ragged(own, NC, FD * N_TM, FD * N_TM // 4, 2))(jax.random.split(arg_keys[1], GROUPS)).reshape((GROUPS, NC)).astype(jnp.int32),
        "w_time": bell_draw(arg_keys[2], (KT, C, C), (3 * C) ** -0.5, 0.15625, ((1, 8),)),
        "w_down": bell_draw(arg_keys[3], (KT, C, C), (3 * C) ** -0.5, 0.15625, ((1, 8),)),
        "cotangent": bell_draw(arg_keys[4], (GROUPS, HALF, S, C), 1.0, 6.0, ((0, 4), (1, 8))),
    }


def clip_start(lengths_row, frames):
    ends = jnp.cumsum(lengths_row)
    return lax.optimization_barrier(jnp.sum(jnp.where(ends[None, :] <= frames[:, None], lengths_row[None, :], 0), axis=1)).astype(jnp.int32)

def features(x_wide):
    scale = lax.rsqrt(lax.optimization_barrier(jnp.mean(x_wide * x_wide, axis=-1, keepdims=True)) + 1e-06)
    return jax.nn.silu(x_wide * scale)

def project(block, weight):
    shape = block.shape
    flat = jnp.dot(block.reshape(-1, shape[-1]), weight, preferred_element_type=jnp.float32)
    return flat.reshape(shape[:-1] + (weight.shape[1],))

def outer(left, right):
    width = left.shape[-1]
    return jnp.dot(left.reshape(-1, width).T, right.reshape(-1, right.shape[-1]), preferred_element_type=jnp.float32)

def one_group(x_bf, lengths_row, cot, w_time, w_down):
    frame_count = x_bf.shape[0]
    half_count = frame_count // 2
    frames = jnp.arange(frame_count, dtype=jnp.int32)
    starts = clip_start(lengths_row, frames)
    x_wide = x_bf.astype(jnp.float32)
    h_in = features(x_wide).astype(jnp.bfloat16)
    zero_rim = jnp.zeros((2,) + h_in.shape[1:], jnp.bfloat16)
    h_ext = jnp.concatenate([zero_rim, h_in], axis=0)
    mixed = x_wide
    time_taps = []
    for offset in range(3):
        valid = frames - offset >= starts
        tapped = jnp.where(valid[:, None, None], h_ext[2 - offset:2 - offset + frame_count], jnp.zeros((), jnp.bfloat16))
        time_taps.append(tapped)
        mixed = mixed + project(tapped, w_time[offset])
    hidden = mixed.astype(jnp.bfloat16)
    out_frames = 2 * jnp.arange(half_count, dtype=jnp.int32)
    out_starts = clip_start(lengths_row, out_frames)
    hidden_ext = jnp.concatenate([zero_rim, hidden], axis=0)
    reduced = jnp.zeros((half_count,) + hidden.shape[1:], jnp.float32)
    down_taps = []
    for offset in range(3):
        valid = out_frames - offset >= out_starts
        tapped = jnp.where(valid[:, None, None], hidden_ext[2 - offset:2 - offset + frame_count][::2], jnp.zeros((), jnp.bfloat16))
        down_taps.append(tapped)
        reduced = reduced + project(tapped, w_down[offset])
    grad_down = jnp.stack([outer(down_taps[offset], cot) for offset in range(3)])
    grad_hidden = jnp.zeros(x_wide.shape, jnp.float32)
    for offset in range(3):
        valid = out_frames - offset >= out_starts
        spread = jnp.where(valid[:, None, None], project(cot, w_down[offset].T), jnp.zeros((), jnp.float32))
        placed = jnp.stack([spread, jnp.zeros_like(spread)], axis=1).reshape((frame_count,) + spread.shape[1:])
        placed = jnp.concatenate([placed, jnp.zeros((2,) + spread.shape[1:], jnp.float32)], axis=0)
        grad_hidden = grad_hidden + placed[offset:offset + frame_count]
    grad_mixed = grad_hidden.astype(jnp.bfloat16)
    grad_time = jnp.stack([outer(time_taps[offset], grad_mixed) for offset in range(3)])
    grad_ext = jnp.concatenate([grad_mixed, zero_rim], axis=0)
    grad_hin = jnp.zeros(x_wide.shape, jnp.float32)
    for offset in range(3):
        valid = frames >= clip_start(lengths_row, frames + offset)
        tapped = jnp.where(valid[:, None, None], grad_ext[offset:offset + frame_count], jnp.zeros((), jnp.bfloat16))
        grad_hin = grad_hin + project(tapped, w_time[offset].T)
    _, pullback = jax.vjp(features, x_wide)
    grad_feat = pullback(grad_hin)[0]
    grad_clips = (grad_hidden + grad_feat).astype(jnp.bfloat16)
    return (reduced.astype(jnp.bfloat16), grad_clips, grad_time, grad_down)

def reference(clips, lengths, w_time, w_down, cotangent):

    def step(carry, items):
        x_bf, lengths_row, cot = items
        reduced, grad_clips, grad_time, grad_down = one_group(x_bf, lengths_row, cot, w_time, w_down)
        return ((carry[0] + grad_time, carry[1] + grad_down), (reduced, grad_clips))
    start_sums = (jnp.zeros(w_time.shape, jnp.float32), jnp.zeros(w_down.shape, jnp.float32))
    sums, stacked = lax.scan(step, start_sums, (clips, lengths, cotangent))
    return (stacked[0], stacked[1], sums[0], sums[1])
```

```python
import functools

import jax
import jax.numpy as jnp
from jax import lax
from jax.experimental import pallas as pl
from jax.experimental.pallas import tpu as pltpu
from jax.sharding import PartitionSpec as P

EPS = 1e-06
VMEM = pl.BlockSpec(memory_space=pltpu.VMEM)
SMEM = pl.BlockSpec(memory_space=pltpu.SMEM)
F32 = jnp.float32
BF16 = jnp.bfloat16


def xor_step(value, axis, distance):
    count = lax.axis_size(axis)
    return lax.ppermute(value, axis, [(i, i ^ distance) for i in range(count)])


def shifted(block, axis, distance):
    devices = range(lax.axis_size(axis))
    route = [(i - distance, i) for i in devices if i - distance in devices]
    return lax.ppermute(block, axis, route)


def dot(left, right):
    return jnp.dot(left, right, preferred_element_type=F32)


def dot_t(left, right):
    return lax.dot_general(left, right, (((1,), (1,)), ((), ())), preferred_element_type=F32)


def kept(flag, block):
    return jnp.where(flag > 0, block, jnp.zeros((), block.dtype))


def live(meta, tap, frame, frames):
    return meta[1 + (tap - 1) * (frames + 3) + frame]


def block_index(meta, apart, other):
    me = meta[0]
    chip, core = me // 2, me % 2
    side = (1 - core) if other else core
    return (chip ^ apart) * 2 + side


def assemble(meta, own, other, full):
    chips, taps, rows, _ = own.shape
    for apart in range(chips):
        for side, source in ((False, own), (True, other)):
            at = pl.multiple_of(block_index(meta, apart, side) * rows, rows)
            for tap in range(taps):
                full[tap, pl.ds(at, rows), :] = source[apart, tap]


def place_rows(meta, chips, rows, values, target, columns):
    for apart in range(chips):
        for side in (False, True):
            at = pl.multiple_of(block_index(meta, apart, side) * rows, rows)
            to = (apart + (chips if side else 0)) * rows
            target[to:to + rows, columns] = values[pl.ds(at, rows), :]


def features_kernel(meta, clips, h_out, ht_out, flip, *, chips, rows):
    x = clips[0].astype(F32)
    scale = lax.rsqrt(jnp.mean(x * x, axis=-1, keepdims=True) + EPS)
    v = x * scale
    h = (v * jax.nn.sigmoid(v)).astype(BF16)
    h_out[0] = h
    flip[...] = h.T
    place_rows(meta, chips, rows, flip, ht_out, slice(None))


def split_rows(value, keep, send, tap):
    chips, _, rows, _ = keep.shape
    for apart in range(chips):
        keep[apart, tap] = value[apart * rows:(apart + 1) * rows]
        to = (chips + apart) * rows
        send[apart, tap] = value[to:to + rows].astype(BF16)


def backward_kernel(meta, cot, cot_next, own, other, ht, gh, gm, keep, send, w, c0, c1, c2, m1, m2):
    half, cells, _ = cot.shape
    frames = 2 * half
    assemble(meta, own, other, w)

    def cot_at(j):
        return cot[j] if j < half else cot_next[j - half]

    for m in range(half + 1):
        here = slice(m * cells, (m + 1) * cells)
        c0[here] = cot_at(m)
        ahead = cot_at(m + 1)
        c1[here] = kept(live(meta, 1, 2 * m + 2, frames), ahead)
        c2[here] = kept(live(meta, 2, 2 * m + 2, frames), ahead)
    odd = dot_t(c1[...], w[1])
    for m in range(half + 1):
        here = odd[m * cells:(m + 1) * cells]
        gm[2 * m + 1] = here.astype(BF16)
        if m < half:
            gh[2 * m + 1] = here
    even = dot_t(c0[...], w[0]) + dot_t(c2[...], w[2])
    for m in range(half + 1):
        here = even[m * cells:(m + 1) * cells]
        gm[2 * m] = here.astype(BF16)
        if m < half:
            gh[2 * m] = here
    for g in range(frames):
        here = slice(g * cells, (g + 1) * cells)
        m1[here] = kept(live(meta, 1, g + 1, frames), gm[g + 1])
        m2[here] = kept(live(meta, 2, g + 2, frames), gm[g + 2])
    flat = gm[0:frames].reshape(frames * cells, gm.shape[-1])
    split_rows(dot(ht[...], flat), keep, send, 0)
    split_rows(dot(ht[...], m1[...]), keep, send, 1)
    split_rows(dot(ht[...], m2[...]), keep, send, 2)


def forward_kernel(meta, clips, h_before, h, cot, cot_next, own, other, hidden, keep, send, w, t1, t2, flip, even_t, odd_t, c1, c2):
    frames, cells, width = clips.shape
    half = frames // 2
    chips, _, rows, _ = own.shape
    assemble(meta, own, other, w)

    def h_at(f):
        return h[f] if f >= 0 else h_before[f + 2]

    def cot_at(j):
        return cot[j] if j < half else cot_next[j - half]

    for f in range(frames):
        here = slice(f * cells, (f + 1) * cells)
        t1[here] = kept(live(meta, 1, f, frames), h_at(f - 1))
        t2[here] = kept(live(meta, 2, f, frames), h_at(f - 2))
    for j in range(half):
        here = slice(j * cells, (j + 1) * cells)
        c1[here] = kept(live(meta, 1, 2 * j + 2, frames), cot_at(j + 1))
        c2[here] = kept(live(meta, 2, 2 * j + 2, frames), cot_at(j + 1))
    flat = h[...].reshape(frames * cells, width)
    mixed = dot(flat, w[0]) + dot(t1[...], w[1]) + dot(t2[...], w[2])
    for f in range(frames):
        value = (clips[f].astype(F32) + mixed[f * cells:(f + 1) * cells]).astype(BF16)
        hidden[f] = value
        flip[...] = value.T
        columns = slice(f // 2 * cells, (f // 2 + 1) * cells)
        place_rows(meta, chips, rows, flip, odd_t if f % 2 else even_t, columns)
    flat_cot = cot[...].reshape(half * cells, width)
    split_rows(dot(even_t[...], flat_cot), keep, send, 0)
    split_rows(dot(odd_t[...], c1[...]), keep, send, 1)
    split_rows(dot(even_t[...], c2[...]), keep, send, 2)


def reduced_kernel(meta, before, hidden, own, other, reduced, w, t0, t1, t2):
    frames, cells, width = hidden.shape
    half = frames // 2
    assemble(meta, own, other, w)
    for j in range(half):
        here = slice(j * cells, (j + 1) * cells)
        t0[here] = hidden[2 * j]
        t1[here] = kept(live(meta, 1, 2 * j, frames), hidden[2 * j - 1] if j else before[1])
        t2[here] = kept(live(meta, 2, 2 * j, frames), hidden[2 * j - 2] if j else before[0])
    out = dot(t0[...], w[0]) + dot(t1[...], w[1]) + dot(t2[...], w[2])
    for j in range(half):
        reduced[j] = out[j * cells:(j + 1) * cells].astype(BF16)


def clips_kernel(meta, clips, gh, gm, own, other, out, w, m1, m2):
    frames, cells, width = clips.shape
    assemble(meta, own, other, w)
    for g in range(frames):
        here = slice(g * cells, (g + 1) * cells)
        m1[here] = kept(live(meta, 1, g + 1, frames), gm[g + 1])
        m2[here] = kept(live(meta, 2, g + 2, frames), gm[g + 2])
    flat = gm[0:frames].reshape(frames * cells, width)
    grad = dot_t(flat, w[0]) + dot_t(m1[...], w[1]) + dot_t(m2[...], w[2])
    for f in range(frames):
        g = grad[f * cells:(f + 1) * cells]
        x = clips[f].astype(F32)
        scale = lax.rsqrt(jnp.mean(x * x, axis=-1, keepdims=True) + EPS)
        v = x * scale
        gate = jax.nn.sigmoid(v)
        gv = g * (gate + v * gate * (1.0 - gate))
        along = jnp.mean(gv * x, axis=-1, keepdims=True)
        out[f] = (gh[f] + scale * gv - (scale * scale * scale) * along * x).astype(BF16)


def shards(clips, lengths, w_time, w_down, cotangent):
    x = clips[0]
    cot = cotangent[0]
    frames, cells, width = x.shape
    half = frames // 2
    devices = lax.axis_size("tm")
    chips = devices // 2
    taps, rows, _ = w_time.shape
    me = lax.axis_index("tm")
    params = pltpu.CompilerParams(vmem_limit_bytes=48 * 1024 * 1024)

    def sds(shape, dtype):
        return jax.ShapeDtypeStruct(shape, dtype)

    def scratch(shape, dtype=BF16):
        return pltpu.VMEM(shape, dtype)

    ends = jnp.cumsum(lengths[0])
    local = me * frames + jnp.arange(-2, frames + 3, dtype=jnp.int32)
    clip = jnp.sum((ends[None, :] <= local[:, None]).astype(jnp.int32), axis=1)
    clip = jnp.where(local < 0, -1, clip)
    live_1 = (clip[2:] == clip[1:-1]).astype(jnp.int32)
    live_2 = (clip[2:] == clip[:-2]).astype(jnp.int32)
    meta = jnp.concatenate([me[None].astype(jnp.int32), live_1, live_2])

    def gathered(weight):
        own = jnp.stack([weight] + [xor_step(weight, "tm", 2 * d) for d in range(1, chips)])
        return own, xor_step(own, "tm", 1)

    cot_next = shifted(cot[:2], "tm", -1)
    down_own, down_other = gathered(w_down)

    h, ht = pl.pallas_call(
        functools.partial(features_kernel, chips=chips, rows=rows),
        grid=(frames,),
        in_specs=[SMEM, pl.BlockSpec((1, cells, width), lambda f: (f, 0, 0))],
        out_specs=(
            pl.BlockSpec((1, cells, width), lambda f: (f, 0, 0)),
            pl.BlockSpec((width, cells), lambda f: (0, f)),
        ),
        out_shape=(sds((frames, cells, width), BF16), sds((width, frames * cells), BF16)),
        scratch_shapes=[scratch((width, cells))],
        name="features",
    )(meta, x)
    h_before = shifted(h[frames - 2:], "tm", 1)

    weight_scratch = scratch((taps, width, width))
    wide = sds((chips, taps, rows, width), F32)
    narrow = sds((chips, taps, rows, width), BF16)
    lot = frames * cells
    gh, gm, time_keep, time_send = pl.pallas_call(
        backward_kernel,
        in_specs=[SMEM] + [VMEM] * 5,
        out_specs=(VMEM,) * 4,
        out_shape=(sds((frames, cells, width), F32), sds((frames + 2, cells, width), BF16), wide, narrow),
        scratch_shapes=[weight_scratch] + [scratch(((half + 1) * cells, width))] * 3 + [scratch((lot, width))] * 2,
        compiler_params=params,
        name="backward",
    )(meta, cot, cot_next, down_own, down_other, ht)

    time_own, time_other = gathered(w_time)
    hidden, down_keep, down_send = pl.pallas_call(
        forward_kernel,
        in_specs=[SMEM] + [VMEM] * 7,
        out_specs=(VMEM,) * 3,
        out_shape=(sds((frames, cells, width), BF16), wide, narrow),
        scratch_shapes=[weight_scratch] + [scratch((lot, width))] * 2
        + [scratch((width, cells))] + [scratch((width, half * cells))] * 2 + [scratch((half * cells, width))] * 2,
        compiler_params=params,
        name="forward",
    )(meta, x, h_before, h, cot, cot_next, time_own, time_other)

    def summed(keep, send):
        part = keep + xor_step(send, "tm", 1).astype(F32)
        total = part[0]
        for d in range(1, chips):
            total = total + xor_step(part[d].astype(BF16), "tm", 2 * d).astype(F32)
        step = 1
        while step < lax.axis_size("group"):
            mine = total.astype(BF16)
            total = mine.astype(F32) + xor_step(mine, "group", step).astype(F32)
            step *= 2
        return total

    grad_time = summed(time_keep, time_send)
    grad_down = summed(down_keep, down_send)

    grad_clips = pl.pallas_call(
        clips_kernel,
        in_specs=[SMEM] + [VMEM] * 5,
        out_specs=VMEM,
        out_shape=sds((frames, cells, width), BF16),
        scratch_shapes=[weight_scratch] + [scratch((lot, width))] * 2,
        compiler_params=params,
        name="clips",
    )(meta, x, gh, gm, time_own, time_other)

    before = shifted(hidden[frames - 2:], "tm", 1)
    reduced = pl.pallas_call(
        reduced_kernel,
        in_specs=[SMEM] + [VMEM] * 4,
        out_specs=VMEM,
        out_shape=sds((half, cells, width), BF16),
        scratch_shapes=[weight_scratch] + [scratch((half * cells, width))] * 3,
        compiler_params=params,
        name="reduced",
    )(meta, before, hidden, down_own, down_other)
    return reduced[None], grad_clips[None], grad_time, grad_down


def solution(mesh):
    in_specs = (
        P("group", "tm", None, None),
        P("group", None),
        P(None, "tm", None),
        P(None, "tm", None),
        P("group", "tm", None, None),
    )
    out_specs = (
        P("group", "tm", None, None),
        P("group", "tm", None, None),
        P(None, "tm", None),
        P(None, "tm", None),
    )
    return jax.shard_map(shards, mesh=mesh, in_specs=in_specs, out_specs=out_specs, check_vma=False)
```

```python
import functools

import jax
import jax.numpy as jnp
from jax import lax
from jax.experimental import pallas as pl
from jax.experimental.pallas import tpu as pltpu
from jax.sharding import PartitionSpec as P

EPS = 1e-06
DOWN, TIME = 0, 1
FEATURES_COST = 20_000_000_000
VMEM = pl.BlockSpec(memory_space=pltpu.VMEM)
SMEM = pl.BlockSpec(memory_space=pltpu.SMEM)
F32 = jnp.float32
BF16 = jnp.bfloat16


def bits_of(count):
    bits = []
    while 1 << len(bits) < count:
        bits.append(1 << len(bits))
    return bits


def exchange(value, step, name):
    bits = bits_of(lax.axis_size("tm"))[1:]
    turn = [bits[step], bits[(step + 1) % len(bits)]]
    with jax.named_scope(f"{name}_tm_{step}"):
        route = [(i, i ^ turn[i % 2]) for i in range(lax.axis_size("tm"))]
        return lax.ppermute(value, "tm", route)


def core_swap(value, name):
    with jax.named_scope(f"{name}_tm_core"):
        return lax.ppermute(value, "tm", [(i, i ^ 1) for i in range(lax.axis_size("tm"))])


def group_exchange(value, step, name):
    groups = lax.axis_size("group")
    bits = bits_of(groups)
    turn = [bits[step], bits[(step + len(bits) // 2) % len(bits)]]
    route = [
        (t * groups + g, t * groups + (g ^ turn[t % 2]))
        for t in range(lax.axis_size("tm"))
        for g in range(groups)
    ]
    with jax.named_scope(f"{name}_group_{step}"):
        return lax.ppermute(value, ("tm", "group"), route)


def shifted(block, axis, distance):
    devices = range(lax.axis_size(axis))
    route = [(i - distance, i) for i in devices if i - distance in devices]
    with jax.named_scope(f"halo_{axis}{distance}_{block.shape[0]}"):
        return lax.ppermute(block, axis, route)


def after(value, *earlier):
    return lax.optimization_barrier((value,) + earlier)[0]


def dot(left, right):
    return jnp.dot(left, right, preferred_element_type=F32)


def dot_t(left, right):
    return lax.dot_general(left, right, (((1,), (1,)), ((), ())), preferred_element_type=F32)


def kept(flag, block):
    return jnp.where(flag > 0, block, jnp.zeros((), block.dtype))


def live(meta, tap, frame, frames):
    return meta[1 + (tap - 1) * (frames + 3) + frame]


def chip_bit(step, count, core):
    return jnp.where(core == 0, 1 << step, 1 << ((step + 1) % count))


def apart(position, chips, core, last_first):
    count = len(bits_of(chips))
    total = 0
    for step in range(count):
        place = count - 1 - step if last_first else step
        if position >> place & 1:
            total = total ^ chip_bit(step, count, core)
    return total


def block_at(meta, position, chips, rows, other, last_first):
    chip, core = meta[0] // 2, meta[0] % 2
    core = 1 - core if other else core
    block = (chip ^ apart(position, chips, core, last_first)) * 2 + core
    return pl.multiple_of(block * rows, rows)


def assemble(meta, refs, which, full):
    early = next(i for i, ref in enumerate(refs) if len(ref.shape) == 4)
    pieces = list(refs[:early]) + [refs[early].at[which * early + i] for i in range(early)]
    for ref in refs[early + 1:]:
        pieces += [ref.at[i] for i in range(early)] if len(ref.shape) == 4 else [ref]
    taps, rows, _ = pieces[0].shape
    chips = len(pieces) // 2
    for index, source in enumerate(pieces):
        at = block_at(meta, index % chips, chips, rows, index >= chips, False)
        for tap in range(taps):
            full[tap, pl.ds(at, rows), :] = source[tap]


def place_rows(meta, chips, rows, values, target, columns):
    for index in range(2 * chips):
        at = block_at(meta, index % chips, chips, rows, index >= chips, True)
        target[index * rows:(index + 1) * rows, columns] = values[pl.ds(at, rows), :]


def split_rows(value, shares, tap):
    half, _, rows, _ = shares[0].shape
    for index in range(4 * half):
        part = value[index * rows:(index + 1) * rows]
        if index < 2 * half:
            shares[index // half][index % half, tap] = part
        elif len(shares) == 3:
            shares[2][index - 2 * half, tap] = part.astype(BF16)
        else:
            shares[2 + index - 2 * half][tap] = part.astype(BF16)


def features(x):
    x = x.astype(F32)
    scale = lax.rsqrt(jnp.mean(x * x, axis=-1, keepdims=True) + EPS)
    v = x * scale
    return (v * jax.nn.sigmoid(v)).astype(BF16)


def features_kernel(meta, clips, h_out, ht_out, flip, *, chips, rows):
    h = features(clips[0])
    h_out[0] = h
    flip[...] = h.T
    place_rows(meta, chips, rows, flip, ht_out, slice(None))


def backward_kernel(meta, cot, cot_next, ht, *refs):
    *pieces, gh, gm, low, high, send, w, c0, c1, c2, m1, m2 = refs
    shares = (low, high, send)
    half, cells, _ = cot.shape
    frames = 2 * half
    assemble(meta, pieces, DOWN, w)

    def cot_at(j):
        return cot[j] if j < half else cot_next[j - half]

    for m in range(half + 1):
        here = slice(m * cells, (m + 1) * cells)
        c0[here] = cot_at(m)
        ahead = cot_at(m + 1)
        c1[here] = kept(live(meta, 1, 2 * m + 2, frames), ahead)
        c2[here] = kept(live(meta, 2, 2 * m + 2, frames), ahead)
    odd = dot_t(c1[...], w[1])
    for m in range(half + 1):
        here = odd[m * cells:(m + 1) * cells]
        gm[2 * m + 1] = here.astype(BF16)
        if m < half:
            gh[2 * m + 1] = here
    even = dot_t(c0[...], w[0]) + dot_t(c2[...], w[2])
    for m in range(half + 1):
        here = even[m * cells:(m + 1) * cells]
        gm[2 * m] = here.astype(BF16)
        if m < half:
            gh[2 * m] = here
    for g in range(frames):
        here = slice(g * cells, (g + 1) * cells)
        m1[here] = kept(live(meta, 1, g + 1, frames), gm[g + 1])
        m2[here] = kept(live(meta, 2, g + 2, frames), gm[g + 2])
    flat = gm[0:frames].reshape(frames * cells, gm.shape[-1])
    split_rows(dot(ht[...], flat), shares, 0)
    split_rows(dot(ht[...], m1[...]), shares, 1)
    split_rows(dot(ht[...], m2[...]), shares, 2)


def forward_kernel(meta, clips, before, h, cot, cot_next, *refs, chips):
    w, t1, t2, flip, even_t, odd_t, c1, c2 = refs[-8:]
    *pieces, hidden, tail = refs[:-10 - chips]
    shares = refs[-10 - chips:-8]
    frames, cells, width = clips.shape
    half = frames // 2
    rows = shares[0].shape[2]
    assemble(meta, pieces, TIME, w)

    h_before = [features(before[0]), features(before[1])]

    def h_at(f):
        return h[f] if f >= 0 else h_before[f + 2]

    def cot_at(j):
        return cot[j] if j < half else cot_next[j - half]

    for f in range(frames):
        here = slice(f * cells, (f + 1) * cells)
        t1[here] = kept(live(meta, 1, f, frames), h_at(f - 1))
        t2[here] = kept(live(meta, 2, f, frames), h_at(f - 2))
    for j in range(half):
        here = slice(j * cells, (j + 1) * cells)
        c1[here] = kept(live(meta, 1, 2 * j + 2, frames), cot_at(j + 1))
        c2[here] = kept(live(meta, 2, 2 * j + 2, frames), cot_at(j + 1))
    flat = h[...].reshape(frames * cells, width)
    mixed = dot(flat, w[0]) + dot(t1[...], w[1]) + dot(t2[...], w[2])
    for f in range(frames):
        value = (clips[f].astype(F32) + mixed[f * cells:(f + 1) * cells]).astype(BF16)
        hidden[f] = value
        if f >= frames - 2:
            tail[f - frames + 2] = value
        flip[...] = value.T
        columns = slice(f // 2 * cells, (f // 2 + 1) * cells)
        place_rows(meta, chips, rows, flip, odd_t if f % 2 else even_t, columns)
    flat_cot = cot[...].reshape(half * cells, width)
    split_rows(dot(even_t[...], flat_cot), shares, 0)
    split_rows(dot(odd_t[...], c1[...]), shares, 1)
    split_rows(dot(even_t[...], c2[...]), shares, 2)


def reduced_kernel(meta, before, hidden, *refs):
    *pieces, reduced, w, t0, t1, t2 = refs
    frames, cells, width = hidden.shape
    half = frames // 2
    assemble(meta, pieces, DOWN, w)
    for j in range(half):
        here = slice(j * cells, (j + 1) * cells)
        t0[here] = hidden[2 * j]
        t1[here] = kept(live(meta, 1, 2 * j, frames), hidden[2 * j - 1] if j else before[1])
        t2[here] = kept(live(meta, 2, 2 * j, frames), hidden[2 * j - 2] if j else before[0])
    out = dot(t0[...], w[0]) + dot(t1[...], w[1]) + dot(t2[...], w[2])
    for j in range(half):
        reduced[j] = out[j * cells:(j + 1) * cells].astype(BF16)


def clips_kernel(meta, clips, gh, gm, *refs):
    *pieces, out, w, m1, m2 = refs
    frames, cells, width = clips.shape
    assemble(meta, pieces, TIME, w)
    for g in range(frames):
        here = slice(g * cells, (g + 1) * cells)
        m1[here] = kept(live(meta, 1, g + 1, frames), gm[g + 1])
        m2[here] = kept(live(meta, 2, g + 2, frames), gm[g + 2])
    flat = gm[0:frames].reshape(frames * cells, width)
    grad = dot_t(flat, w[0]) + dot_t(m1[...], w[1]) + dot_t(m2[...], w[2])
    for f in range(frames):
        g = grad[f * cells:(f + 1) * cells]
        x = clips[f].astype(F32)
        scale = lax.rsqrt(jnp.mean(x * x, axis=-1, keepdims=True) + EPS)
        v = x * scale
        gate = jax.nn.sigmoid(v)
        gv = g * (gate + v * gate * (1.0 - gate))
        along = jnp.mean(gv * x, axis=-1, keepdims=True)
        out[f] = (gh[f] + scale * gv - (scale * scale * scale) * along * x).astype(BF16)


def shards(clips, lengths, w_time, w_down, cotangent):
    x = clips[0]
    cot = cotangent[0]
    frames, cells, width = x.shape
    half = frames // 2
    devices = lax.axis_size("tm")
    chips = devices // 2
    early = chips // 2
    last = len(bits_of(chips)) - 1
    taps, rows, _ = w_time.shape
    me = lax.axis_index("tm")
    lot = frames * cells

    def sds(shape, dtype=BF16):
        return jax.ShapeDtypeStruct(shape, dtype)

    def scratch(*shape):
        return pltpu.VMEM(shape, BF16)

    def call(kernel, name, inputs, outs, scratches):
        tree = (VMEM,) * len(outs) if isinstance(outs, tuple) else VMEM
        return pl.pallas_call(
            kernel,
            in_specs=[SMEM] + [VMEM] * (len(inputs) - 1),
            out_specs=tree,
            out_shape=outs,
            scratch_shapes=scratches,
            compiler_params=pltpu.CompilerParams(vmem_limit_bytes=36 * 1024 * 1024),
            cost_estimate=pl.CostEstimate(flops=1_000_000, bytes_accessed=1000, transcendentals=0),
            name=name,
        )(*inputs)

    ends = jnp.cumsum(lengths[0])
    local = me * frames + jnp.arange(-2, frames + 3, dtype=jnp.int32)
    clip = jnp.sum((ends[None, :] <= local[:, None]).astype(jnp.int32), axis=1)
    clip = jnp.where(local < 0, -1, clip)
    live_1 = (clip[2:] == clip[1:-1]).astype(jnp.int32)
    live_2 = (clip[2:] == clip[:-2]).astype(jnp.int32)
    meta = jnp.concatenate([me[None].astype(jnp.int32), live_1, live_2])

    down, time = [w_down], [w_time]
    for step in range(last):
        earlier = down[1:] + time[1:]
        down = down + [exchange(after(part, *earlier), step, "down") for part in down]
        time = time + [exchange(after(part, *earlier), step, "time") for part in time]
    first = down[1:] + time[1:]
    late = jnp.stack(down + time)
    cot_next = shifted(after(cot[:2], late), "tm", -1)
    x_before = shifted(after(x[frames - 2:], late), "tm", 1)
    late = exchange(late, last, "late")
    down_other = [core_swap(part, "down") for part in down]
    time_other = [core_swap(part, "time") for part in time]

    h, ht = pl.pallas_call(
        functools.partial(features_kernel, chips=chips, rows=rows),
        grid=(frames,),
        in_specs=[SMEM, pl.BlockSpec((1, cells, width), lambda f: (f, 0, 0))],
        out_specs=(
            pl.BlockSpec((1, cells, width), lambda f: (f, 0, 0)),
            pl.BlockSpec((width, cells), lambda f: (0, f)),
        ),
        out_shape=(sds((frames, cells, width)), sds((width, lot))),
        scratch_shapes=[scratch(width, cells)],
        compiler_params=pltpu.CompilerParams(vmem_limit_bytes=36 * 1024 * 1024),
        cost_estimate=pl.CostEstimate(flops=FEATURES_COST, bytes_accessed=1000, transcendentals=0),
        name="features",
    )(after(meta, *first, *down_other, *time_other), x)

    late = after(late, h)
    down = down + [late] + down_other + [core_swap(late[i], "down") for i in range(early)]
    time_late = core_swap(late[early:], "time")

    shares = (
        sds((early, taps, rows, width), F32),
        sds((early, taps, rows, width), F32),
        sds((chips, taps, rows, width)),
    )
    full = scratch(taps, width, width)
    gh, gm, *time_shares = call(
        backward_kernel,
        "backward",
        [after(meta, x_before), cot, cot_next, ht] + down,
        (sds((frames, cells, width), F32), sds((frames + 2, cells, width))) + shares,
        [full] + [scratch((half + 1) * cells, width)] * 3 + [scratch(lot, width)] * 2,
    )

    def core_sum(shares, name, *earlier):
        low, high, *send = shares
        if len(send) == 1:
            other = after(core_swap(send[0], name), *earlier)
        else:
            other = jnp.stack([after(core_swap(part, name), *earlier) for part in send])
        other = other.astype(F32)
        return low + other[:early], (high + other[early:]).astype(BF16)

    def plane_step(low, other):
        total = low + other.astype(F32)
        count = total.shape[0] // 2
        return total[:count], total[count:].astype(BF16)

    def group_sum(mine, step, name):
        return mine.astype(F32) + group_exchange(mine, step, name).astype(F32)

    time = time + [late] + time_other + [time_late]
    low_time, high_time = core_sum(time_shares, "grad_time")
    hidden, tail, *down_shares = call(
        functools.partial(forward_kernel, chips=chips),
        "forward",
        [after(meta, high_time), x, x_before, h, cot, cot_next] + time,
        (sds((frames, cells, width)), sds((2, cells, width))) + shares[:2]
        + (sds((taps, rows, width)),) * chips,
        [full] + [scratch(lot, width)] * 2 + [scratch(width, cells)]
        + [scratch(width, half * cells)] * 2 + [scratch(half * cells, width)] * 2,
    )

    for step in range(last):
        other = after(exchange(high_time, step, "grad_time"), hidden)
        low_time, high_time = plane_step(low_time, other)
        if step == 0:
            low_down, high_down = core_sum(down_shares, "grad_down", high_time)
            grad_clips = call(
                clips_kernel,
                "clips",
                [after(meta, high_down), x, gh, gm] + time,
                sds((frames, cells, width)),
                [full] + [scratch(lot, width)] * 2,
            )
        other = after(exchange(high_down, step, "grad_down"), grad_clips)
        low_down, high_down = plane_step(low_down, other)

    other = after(exchange(high_time, last, "grad_time"), high_down)
    mine_time = (low_time[0] + other[0].astype(F32)).astype(BF16)
    before = shifted(after(tail, mine_time), "tm", 1)
    other = after(exchange(high_down, last, "grad_down"), mine_time)
    mine_down = (low_down[0] + other[0].astype(F32)).astype(BF16)
    reduced = call(
        reduced_kernel,
        "reduced",
        [after(meta, mine_down), before, hidden] + down,
        sds((half, cells, width)),
        [full] + [scratch(half * cells, width)] * 3,
    )
    steps = len(bits_of(lax.axis_size("group")))
    for step in range(steps):
        grad_time = mine_time.astype(F32) + after(group_exchange(mine_time, step, "grad_time"), reduced).astype(F32)
        if step < steps - 1:
            mine_time = grad_time.astype(BF16)
        grad_down = mine_down.astype(F32) + after(group_exchange(mine_down, step, "grad_down"), mine_time).astype(F32)
        if step < steps - 1:
            mine_down = grad_down.astype(BF16)
    return reduced[None], grad_clips[None], grad_time, grad_down


def solution(mesh):
    in_specs = (
        P("group", "tm", None, None),
        P("group", None),
        P(None, "tm", None),
        P(None, "tm", None),
        P("group", "tm", None, None),
    )
    out_specs = (
        P("group", "tm", None, None),
        P("group", "tm", None, None),
        P(None, "tm", None),
        P(None, "tm", None),
    )
    return jax.shard_map(shards, mesh=mesh, in_specs=in_specs, out_specs=out_specs, check_vma=False)
```

```python
import functools

import jax
import jax.numpy as jnp
from jax import lax
from jax.experimental import pallas as pl
from jax.experimental.pallas import tpu as pltpu
from jax.sharding import PartitionSpec as P

EPS = 1e-06
FEATURES_COST = 20_000_000_000
VMEM = pl.BlockSpec(memory_space=pltpu.VMEM)
SMEM = pl.BlockSpec(memory_space=pltpu.SMEM)
F32 = jnp.float32
BF16 = jnp.bfloat16


def bits_of(count):
    bits = []
    while 1 << len(bits) < count:
        bits.append(1 << len(bits))
    return bits


def exchange(value, step, name):
    bits = bits_of(lax.axis_size("tm"))[1:]
    turn = [bits[step], bits[(step + 1) % len(bits)]]
    with jax.named_scope(f"{name}_tm_{step}"):
        route = [(i, i ^ turn[i % 2]) for i in range(lax.axis_size("tm"))]
        return lax.ppermute(value, "tm", route)


def core_swap(value, name):
    with jax.named_scope(f"{name}_tm_core"):
        return lax.ppermute(value, "tm", [(i, i ^ 1) for i in range(lax.axis_size("tm"))])


def group_exchange(value, step, name):
    groups = lax.axis_size("group")
    bits = bits_of(groups)
    turn = [bits[step], bits[(step + len(bits) // 2) % len(bits)]]
    route = [
        (t * groups + g, t * groups + (g ^ turn[t % 2]))
        for t in range(lax.axis_size("tm"))
        for g in range(groups)
    ]
    with jax.named_scope(f"{name}_group_{step}"):
        return lax.ppermute(value, ("tm", "group"), route)


def shifted(block, axis, distance):
    devices = range(lax.axis_size(axis))
    route = [(i - distance, i) for i in devices if i - distance in devices]
    with jax.named_scope(f"halo_{axis}{distance}_{block.shape[0]}"):
        return lax.ppermute(block, axis, route)


def after(value, *earlier):
    return lax.optimization_barrier((value,) + earlier)[0]


def dot(left, right):
    return jnp.dot(left, right, preferred_element_type=F32)


def dot_t(left, right):
    return lax.dot_general(left, right, (((1,), (1,)), ((), ())), preferred_element_type=F32)


def kept(flag, block):
    return jnp.where(flag > 0, block, jnp.zeros((), block.dtype))


def live(meta, tap, frame, frames):
    return meta[1 + (tap - 1) * (frames + 3) + frame]


def chip_bit(step, count, core):
    return jnp.where(core == 0, 1 << step, 1 << ((step + 1) % count))


def apart(position, chips, core, last_first):
    count = len(bits_of(chips))
    total = 0
    for step in range(count):
        place = count - 1 - step if last_first else step
        if position >> place & 1:
            total = total ^ chip_bit(step, count, core)
    return total


def block_at(meta, position, chips, rows, other, last_first):
    chip, core = meta[0] // 2, meta[0] % 2
    core = 1 - core if other else core
    block = (chip ^ apart(position, chips, core, last_first)) * 2 + core
    return pl.multiple_of(block * rows, rows)


def assemble(meta, pieces, full):
    pieces = [piece for ref in pieces for piece in ([ref.at[i] for i in range(ref.shape[0])] if len(ref.shape) == 4 else [ref])]
    taps, rows, _ = pieces[0].shape
    chips = len(pieces) // 2
    for index, source in enumerate(pieces):
        at = block_at(meta, index % chips, chips, rows, index >= chips, False)
        for tap in range(taps):
            full[tap, pl.ds(at, rows), :] = source[tap]


def place_rows(meta, chips, rows, values, target, columns):
    for index in range(2 * chips):
        at = block_at(meta, index % chips, chips, rows, index >= chips, True)
        target[index * rows:(index + 1) * rows, columns] = values[pl.ds(at, rows), :]


def split_rows(value, shares, tap):
    half, _, rows, _ = shares[0].shape
    for index in range(4 * half):
        part = value[index * rows:(index + 1) * rows]
        if index < 2 * half:
            shares[index // half][index % half, tap] = part
        else:
            shares[2 + index - 2 * half][tap] = part.astype(BF16)


def features(x):
    x = x.astype(F32)
    scale = lax.rsqrt(jnp.mean(x * x, axis=-1, keepdims=True) + EPS)
    v = x * scale
    return (v * jax.nn.sigmoid(v)).astype(BF16)


def features_kernel(meta, clips, h_out, ht_out, flip, *, chips, rows):
    h = features(clips[0])
    h_out[0] = h
    flip[...] = h.T
    place_rows(meta, chips, rows, flip, ht_out, slice(None))


def backward_kernel(meta, cot, cot_next, ht, *refs, chips):
    w, c0, c1, c2, m1, m2 = refs[-6:]
    *pieces, gh, gm = refs[:-8 - chips]
    shares = refs[-8 - chips:-6]
    half, cells, _ = cot.shape
    frames = 2 * half
    assemble(meta, pieces, w)

    def cot_at(j):
        return cot[j] if j < half else cot_next[j - half]

    for m in range(half + 1):
        here = slice(m * cells, (m + 1) * cells)
        c0[here] = cot_at(m)
        ahead = cot_at(m + 1)
        c1[here] = kept(live(meta, 1, 2 * m + 2, frames), ahead)
        c2[here] = kept(live(meta, 2, 2 * m + 2, frames), ahead)
    odd = dot_t(c1[...], w[1])
    for m in range(half + 1):
        here = odd[m * cells:(m + 1) * cells]
        gm[2 * m + 1] = here.astype(BF16)
        if m < half:
            gh[2 * m + 1] = here
    even = dot_t(c0[...], w[0]) + dot_t(c2[...], w[2])
    for m in range(half + 1):
        here = even[m * cells:(m + 1) * cells]
        gm[2 * m] = here.astype(BF16)
        if m < half:
            gh[2 * m] = here
    for g in range(frames):
        here = slice(g * cells, (g + 1) * cells)
        m1[here] = kept(live(meta, 1, g + 1, frames), gm[g + 1])
        m2[here] = kept(live(meta, 2, g + 2, frames), gm[g + 2])
    flat = gm[0:frames].reshape(frames * cells, gm.shape[-1])
    split_rows(dot(ht[...], flat), shares, 0)
    split_rows(dot(ht[...], m1[...]), shares, 1)
    split_rows(dot(ht[...], m2[...]), shares, 2)


def forward_kernel(meta, clips, before, h, cot, cot_next, *refs, chips):
    w, t1, t2, flip, even_t, odd_t, c1, c2 = refs[-8:]
    *pieces, hidden, tail = refs[:-10 - chips]
    shares = refs[-10 - chips:-8]
    frames, cells, width = clips.shape
    half = frames // 2
    rows = shares[0].shape[2]
    assemble(meta, pieces, w)

    h_before = [features(before[0]), features(before[1])]

    def h_at(f):
        return h[f] if f >= 0 else h_before[f + 2]

    def cot_at(j):
        return cot[j] if j < half else cot_next[j - half]

    for f in range(frames):
        here = slice(f * cells, (f + 1) * cells)
        t1[here] = kept(live(meta, 1, f, frames), h_at(f - 1))
        t2[here] = kept(live(meta, 2, f, frames), h_at(f - 2))
    for j in range(half):
        here = slice(j * cells, (j + 1) * cells)
        c1[here] = kept(live(meta, 1, 2 * j + 2, frames), cot_at(j + 1))
        c2[here] = kept(live(meta, 2, 2 * j + 2, frames), cot_at(j + 1))
    flat = h[...].reshape(frames * cells, width)
    mixed = dot(flat, w[0]) + dot(t1[...], w[1]) + dot(t2[...], w[2])
    for f in range(frames):
        value = (clips[f].astype(F32) + mixed[f * cells:(f + 1) * cells]).astype(BF16)
        hidden[f] = value
        if f >= frames - 2:
            tail[f - frames + 2] = value
        flip[...] = value.T
        columns = slice(f // 2 * cells, (f // 2 + 1) * cells)
        place_rows(meta, chips, rows, flip, odd_t if f % 2 else even_t, columns)
    flat_cot = cot[...].reshape(half * cells, width)
    split_rows(dot(even_t[...], flat_cot), shares, 0)
    split_rows(dot(odd_t[...], c1[...]), shares, 1)
    split_rows(dot(even_t[...], c2[...]), shares, 2)


def reduced_kernel(meta, before, hidden, *refs):
    *pieces, reduced, w, t0, t1, t2 = refs
    frames, cells, width = hidden.shape
    half = frames // 2
    assemble(meta, pieces, w)
    for j in range(half):
        here = slice(j * cells, (j + 1) * cells)
        t0[here] = hidden[2 * j]
        t1[here] = kept(live(meta, 1, 2 * j, frames), hidden[2 * j - 1] if j else before[1])
        t2[here] = kept(live(meta, 2, 2 * j, frames), hidden[2 * j - 2] if j else before[0])
    out = dot(t0[...], w[0]) + dot(t1[...], w[1]) + dot(t2[...], w[2])
    for j in range(half):
        reduced[j] = out[j * cells:(j + 1) * cells].astype(BF16)


def clips_kernel(meta, clips, gh, gm, *refs):
    *pieces, out, w, m1, m2 = refs
    frames, cells, width = clips.shape
    assemble(meta, pieces, w)
    for g in range(frames):
        here = slice(g * cells, (g + 1) * cells)
        m1[here] = kept(live(meta, 1, g + 1, frames), gm[g + 1])
        m2[here] = kept(live(meta, 2, g + 2, frames), gm[g + 2])
    flat = gm[0:frames].reshape(frames * cells, width)
    grad = dot_t(flat, w[0]) + dot_t(m1[...], w[1]) + dot_t(m2[...], w[2])
    for f in range(frames):
        g = grad[f * cells:(f + 1) * cells]
        x = clips[f].astype(F32)
        scale = lax.rsqrt(jnp.mean(x * x, axis=-1, keepdims=True) + EPS)
        v = x * scale
        gate = jax.nn.sigmoid(v)
        gv = g * (gate + v * gate * (1.0 - gate))
        along = jnp.mean(gv * x, axis=-1, keepdims=True)
        out[f] = (gh[f] + scale * gv - (scale * scale * scale) * along * x).astype(BF16)


def shards(clips, lengths, w_time, w_down, cotangent):
    x = clips[0]
    cot = cotangent[0]
    frames, cells, width = x.shape
    half = frames // 2
    devices = lax.axis_size("tm")
    chips = devices // 2
    early = chips // 2
    last = len(bits_of(chips)) - 1
    taps, rows, _ = w_time.shape
    me = lax.axis_index("tm")
    lot = frames * cells

    def sds(shape, dtype=BF16):
        return jax.ShapeDtypeStruct(shape, dtype)

    def scratch(*shape):
        return pltpu.VMEM(shape, BF16)

    def call(kernel, name, inputs, outs, scratches):
        tree = (VMEM,) * len(outs) if isinstance(outs, tuple) else VMEM
        return pl.pallas_call(
            kernel,
            in_specs=[SMEM] + [VMEM] * (len(inputs) - 1),
            out_specs=tree,
            out_shape=outs,
            scratch_shapes=scratches,
            compiler_params=pltpu.CompilerParams(vmem_limit_bytes=36 * 1024 * 1024),
            cost_estimate=pl.CostEstimate(flops=1_000_000, bytes_accessed=1000, transcendentals=0),
            name=name,
        )(*inputs)

    ends = jnp.cumsum(lengths[0])
    local = me * frames + jnp.arange(-2, frames + 3, dtype=jnp.int32)
    clip = jnp.sum((ends[None, :] <= local[:, None]).astype(jnp.int32), axis=1)
    clip = jnp.where(local < 0, -1, clip)
    live_1 = (clip[2:] == clip[1:-1]).astype(jnp.int32)
    live_2 = (clip[2:] == clip[:-2]).astype(jnp.int32)
    meta = jnp.concatenate([me[None].astype(jnp.int32), live_1, live_2])

    down, time = [w_down], [w_time]
    for step in range(last):
        down = down + [exchange(part, step, "down") for part in down]
        time = time + [exchange(part, step, "time") for part in time]
    down_own = exchange(w_down, last, "down_own")
    cot_next = shifted(cot[:2], "tm", -1)
    down_late = [exchange(part, last, "down") for part in down[1:]]
    time_late = jnp.stack(time)
    first = [cot_next, down_own] + down[1:] + time[1:]
    time_late = after(time_late, cot_next, *down)
    x_before = shifted(after(x[frames - 2:], time_late), "tm", 1)
    time_late = exchange(time_late, last, "time")
    down = down + [down_own]
    down_other = [core_swap(part, "down") for part in down]
    time_other = [core_swap(part, "time") for part in time]

    h, ht = pl.pallas_call(
        functools.partial(features_kernel, chips=chips, rows=rows),
        grid=(frames,),
        in_specs=[SMEM, pl.BlockSpec((1, cells, width), lambda f: (f, 0, 0))],
        out_specs=(
            pl.BlockSpec((1, cells, width), lambda f: (f, 0, 0)),
            pl.BlockSpec((width, cells), lambda f: (0, f)),
        ),
        out_shape=(sds((frames, cells, width)), sds((width, lot))),
        scratch_shapes=[scratch(width, cells)],
        compiler_params=pltpu.CompilerParams(vmem_limit_bytes=36 * 1024 * 1024),
        cost_estimate=pl.CostEstimate(flops=FEATURES_COST, bytes_accessed=1000, transcendentals=0),
        name="features",
    )(after(meta, *first, *down_late, *down_other, *time_other), x)

    down = down + down_late + down_other + [after(core_swap(part, "down"), h) for part in down_late]

    shares = (
        sds((early, taps, rows, width), F32),
        sds((early, taps, rows, width), F32),
    ) + (sds((taps, rows, width)),) * chips
    full = scratch(taps, width, width)
    gh, gm, *time_shares = call(
        functools.partial(backward_kernel, chips=chips),
        "backward",
        [meta, cot, cot_next, ht] + down,
        (sds((frames, cells, width), F32), sds((frames + 2, cells, width))) + shares,
        [full] + [scratch((half + 1) * cells, width)] * 3 + [scratch(lot, width)] * 2,
    )

    def core_sum(shares, name, *earlier):
        low, high, *send = shares
        other = jnp.stack([after(core_swap(part, name), *earlier) for part in send]).astype(F32)
        return low + other[:early], (high + other[early:]).astype(BF16)

    def plane_step(low, other):
        total = low + other.astype(F32)
        count = total.shape[0] // 2
        return total[:count], total[count:].astype(BF16)

    def group_sum(mine, step, name):
        return mine.astype(F32) + group_exchange(mine, step, name).astype(F32)

    time_late = after(time_late, gm)
    time = time + [time_late] + time_other + [core_swap(time_late, "time")]
    low_time, high_time = core_sum(time_shares, "grad_time", x_before)
    hidden, tail, *down_shares = call(
        functools.partial(forward_kernel, chips=chips),
        "forward",
        [after(meta, high_time), x, x_before, h, cot, cot_next] + time,
        (sds((frames, cells, width)), sds((2, cells, width))) + shares,
        [full] + [scratch(lot, width)] * 2 + [scratch(width, cells)]
        + [scratch(width, half * cells)] * 2 + [scratch(half * cells, width)] * 2,
    )

    for step in range(last):
        other = after(exchange(high_time, step, "grad_time"), hidden)
        low_time, high_time = plane_step(low_time, other)
        if step == 0:
            low_down, high_down = core_sum(down_shares, "grad_down", high_time)
            grad_clips = call(
                clips_kernel,
                "clips",
                [after(meta, high_down), x, gh, gm] + time,
                sds((frames, cells, width)),
                [full] + [scratch(lot, width)] * 2,
            )
        if step == last - 1:
            other = after(exchange(high_time, last, "grad_time"), grad_clips)
            mine_time = (low_time[0] + other[0].astype(F32)).astype(BF16)
            other = after(exchange(high_down, step, "grad_down"), mine_time)
        else:
            other = after(exchange(high_down, step, "grad_down"), grad_clips)
        low_down, high_down = plane_step(low_down, other)
    other = exchange(high_down, last, "grad_down")
    mine_down = (low_down[0] + other[0].astype(F32)).astype(BF16)
    before = shifted(after(tail, mine_down), "tm", 1)
    steps = len(bits_of(lax.axis_size("group")))
    for step in range(steps):
        if step == steps - 1:
            reduced = call(
                reduced_kernel,
                "reduced",
                [after(meta, mine_down), before, hidden] + down,
                sds((half, cells, width)),
                [full] + [scratch(half * cells, width)] * 3,
            )
        done = mine_down if step < steps - 1 else reduced
        grad_time = mine_time.astype(F32) + after(group_exchange(mine_time, step, "grad_time"), done).astype(F32)
        if step < steps - 1:
            mine_time = grad_time.astype(BF16)
        grad_down = mine_down.astype(F32) + after(group_exchange(mine_down, step, "grad_down"), mine_time).astype(F32)
        if step < steps - 1:
            mine_down = grad_down.astype(BF16)
    return reduced[None], grad_clips[None], grad_time, grad_down


def solution(mesh):
    in_specs = (
        P("group", "tm", None, None),
        P("group", None),
        P(None, "tm", None),
        P(None, "tm", None),
        P("group", "tm", None, None),
    )
    out_specs = (
        P("group", "tm", None, None),
        P("group", "tm", None, None),
        P(None, "tm", None),
        P(None, "tm", None),
    )
    return jax.shard_map(shards, mesh=mesh, in_specs=in_specs, out_specs=out_specs, check_vma=False)
```

```python
import functools

import jax
import jax.numpy as jnp
from jax import lax
from jax.experimental import pallas as pl
from jax.experimental.pallas import tpu as pltpu
from jax.sharding import PartitionSpec as P

EPS = 1e-06
PARTS = 2
TAIL = -1
FEATURES_COST = 20_000_000_000
VMEM = pl.BlockSpec(memory_space=pltpu.VMEM)
SMEM = pl.BlockSpec(memory_space=pltpu.SMEM)
F32 = jnp.float32
BF16 = jnp.bfloat16


def bits_of(count):
    bits = []
    while 1 << len(bits) < count:
        bits.append(1 << len(bits))
    return bits


def exchange(value, step, name):
    bits = bits_of(lax.axis_size("tm"))[1:]
    turn = [bits[step], bits[(step + 1) % len(bits)]]
    with jax.named_scope(f"{name}_tm_{step}"):
        route = [(i, i ^ turn[i % 2]) for i in range(lax.axis_size("tm"))]
        return lax.ppermute(value, "tm", route)


def core_swap(value, name):
    with jax.named_scope(f"{name}_tm_core"):
        return lax.ppermute(value, "tm", [(i, i ^ 1) for i in range(lax.axis_size("tm"))])


def group_exchange(value, step, name):
    groups = lax.axis_size("group")
    bits = bits_of(groups)
    turn = [bits[step], bits[(step + len(bits) // 2) % len(bits)]]
    route = [
        (t * groups + g, t * groups + (g ^ turn[t % 2]))
        for t in range(lax.axis_size("tm"))
        for g in range(groups)
    ]
    with jax.named_scope(f"{name}_group_{step}"):
        return lax.ppermute(value, ("tm", "group"), route)


def shifted(block, axis, distance):
    devices = range(lax.axis_size(axis))
    route = [(i - distance, i) for i in devices if i - distance in devices]
    with jax.named_scope(f"halo_{axis}{distance}_{block.shape[0]}"):
        return lax.ppermute(block, axis, route)


def after(value, *earlier):
    return lax.optimization_barrier((value,) + earlier)[0]


def dot(left, right):
    return jnp.dot(left, right, preferred_element_type=F32)


def dot_t(left, right):
    return lax.dot_general(left, right, (((1,), (1,)), ((), ())), preferred_element_type=F32)


def kept(flag, block):
    return jnp.where(flag > 0, block, jnp.zeros((), block.dtype))


def live(meta, tap, frame, frames):
    return meta[1 + (tap - 1) * (frames + 3) + frame]


def chip_bit(step, count, core):
    return jnp.where(core == 0, 1 << step, 1 << ((step + 1) % count))


def apart(position, chips, core, last_first):
    count = len(bits_of(chips))
    total = 0
    for step in range(count):
        place = count - 1 - step if last_first else step
        if position >> place & 1:
            total = total ^ chip_bit(step, count, core)
    return total


def block_at(meta, position, chips, rows, other, last_first):
    chip, core = meta[0] // 2, meta[0] % 2
    core = 1 - core if other else core
    block = (chip ^ apart(position, chips, core, last_first)) * 2 + core
    return pl.multiple_of(block * rows, rows)


def assemble(meta, pieces, full):
    pieces = [piece for ref in pieces for piece in ([ref.at[i] for i in range(ref.shape[0])] if len(ref.shape) == 4 else [ref])]
    taps, rows, _ = pieces[0].shape
    chips = len(pieces) // 2
    for index, source in enumerate(pieces):
        at = block_at(meta, index % chips, chips, rows, index >= chips, False)
        for tap in range(taps):
            full[tap, pl.ds(at, rows), :] = source[tap]


def place_rows(meta, chips, rows, values, target, columns):
    for index in range(2 * chips):
        at = block_at(meta, index % chips, chips, rows, index >= chips, True)
        target[index * rows:(index + 1) * rows, columns] = values[pl.ds(at, rows), :]


def split_rows(value, shares, tap):
    half, _, rows, _ = shares[0].shape
    for index in range(4 * half):
        part = value[index * rows:(index + 1) * rows]
        if index < 2 * half:
            shares[index // half][index % half, tap] = part
        else:
            shares[2 + index - 2 * half][tap] = part.astype(BF16)


def features(x):
    x = x.astype(F32)
    scale = lax.rsqrt(jnp.mean(x * x, axis=-1, keepdims=True) + EPS)
    v = x * scale
    return (v * jax.nn.sigmoid(v)).astype(BF16)


def features_kernel(meta, clips, h_out, ht_out, flip, *, chips, rows):
    h = features(clips[0])
    h_out[0] = h
    flip[...] = h.T
    place_rows(meta, chips, rows, flip, ht_out, slice(None))


def backward_kernel(meta, cot, cot_next, ht, *refs, chips):
    w, c0, c1, c2, m1, m2 = refs[-6:]
    *pieces, gh, gm = refs[:-8 - chips]
    shares = refs[-8 - chips:-6]
    half, cells, _ = cot.shape
    frames = 2 * half
    assemble(meta, pieces, w)

    def cot_at(j):
        return cot[j] if j < half else cot_next[j - half]

    for m in range(half + 1):
        here = slice(m * cells, (m + 1) * cells)
        c0[here] = cot_at(m)
        ahead = cot_at(m + 1)
        c1[here] = kept(live(meta, 1, 2 * m + 2, frames), ahead)
        c2[here] = kept(live(meta, 2, 2 * m + 2, frames), ahead)
    odd = dot_t(c1[...], w[1])
    for m in range(half + 1):
        here = odd[m * cells:(m + 1) * cells]
        gm[2 * m + 1] = here.astype(BF16)
        if m < half:
            gh[2 * m + 1] = here
    even = dot_t(c0[...], w[0]) + dot_t(c2[...], w[2])
    for m in range(half + 1):
        here = even[m * cells:(m + 1) * cells]
        gm[2 * m] = here.astype(BF16)
        if m < half:
            gh[2 * m] = here
    for g in range(frames):
        here = slice(g * cells, (g + 1) * cells)
        m1[here] = kept(live(meta, 1, g + 1, frames), gm[g + 1])
        m2[here] = kept(live(meta, 2, g + 2, frames), gm[g + 2])
    flat = gm[0:frames].reshape(frames * cells, gm.shape[-1])
    split_rows(dot(ht[...], flat), shares, 0)
    split_rows(dot(ht[...], m1[...]), shares, 1)
    split_rows(dot(ht[...], m2[...]), shares, 2)


def forward_kernel(meta, clips, before, h, cot, cot_next, *refs, chips):
    w, t1, t2, flip, even_t, odd_t, c1, c2 = refs[-8:]
    *pieces, hidden, tail = refs[:-10 - chips]
    shares = refs[-10 - chips:-8]
    frames, cells, width = clips.shape
    half = frames // 2
    rows = shares[0].shape[2]
    assemble(meta, pieces, w)

    h_before = [features(before[0]), features(before[1])]

    def h_at(f):
        return h[f] if f >= 0 else h_before[f + 2]

    def cot_at(j):
        return cot[j] if j < half else cot_next[j - half]

    for f in range(frames):
        here = slice(f * cells, (f + 1) * cells)
        t1[here] = kept(live(meta, 1, f, frames), h_at(f - 1))
        t2[here] = kept(live(meta, 2, f, frames), h_at(f - 2))
    for j in range(half):
        here = slice(j * cells, (j + 1) * cells)
        c1[here] = kept(live(meta, 1, 2 * j + 2, frames), cot_at(j + 1))
        c2[here] = kept(live(meta, 2, 2 * j + 2, frames), cot_at(j + 1))
    flat = h[...].reshape(frames * cells, width)
    mixed = dot(flat, w[0]) + dot(t1[...], w[1]) + dot(t2[...], w[2])
    for f in range(frames):
        value = (clips[f].astype(F32) + mixed[f * cells:(f + 1) * cells]).astype(BF16)
        hidden[f] = value
        if f >= frames - 2:
            tail[f - frames + 2] = value
        flip[...] = value.T
        columns = slice(f // 2 * cells, (f // 2 + 1) * cells)
        place_rows(meta, chips, rows, flip, odd_t if f % 2 else even_t, columns)
    flat_cot = cot[...].reshape(half * cells, width)
    split_rows(dot(even_t[...], flat_cot), shares, 0)
    split_rows(dot(odd_t[...], c1[...]), shares, 1)
    split_rows(dot(even_t[...], c2[...]), shares, 2)


def reduced_kernel(meta, before, hidden, *refs):
    *pieces, reduced, w, t0, t1, t2 = refs
    frames, cells, width = hidden.shape
    half = frames // 2
    assemble(meta, pieces, w)
    for j in range(half):
        here = slice(j * cells, (j + 1) * cells)
        t0[here] = hidden[2 * j]
        t1[here] = kept(live(meta, 1, 2 * j, frames), hidden[2 * j - 1] if j else before[1])
        t2[here] = kept(live(meta, 2, 2 * j, frames), hidden[2 * j - 2] if j else before[0])
    out = dot(t0[...], w[0]) + dot(t1[...], w[1]) + dot(t2[...], w[2])
    for j in range(half):
        reduced[j] = out[j * cells:(j + 1) * cells].astype(BF16)


def clips_kernel(meta, clips, gh, gm, *refs):
    *pieces, out, w, m1, m2 = refs
    frames, cells, width = clips.shape
    assemble(meta, pieces, w)
    for g in range(frames):
        here = slice(g * cells, (g + 1) * cells)
        m1[here] = kept(live(meta, 1, g + 1, frames), gm[g + 1])
        m2[here] = kept(live(meta, 2, g + 2, frames), gm[g + 2])
    flat = gm[0:frames].reshape(frames * cells, width)
    grad = dot_t(flat, w[0]) + dot_t(m1[...], w[1]) + dot_t(m2[...], w[2])
    for f in range(frames):
        g = grad[f * cells:(f + 1) * cells]
        x = clips[f].astype(F32)
        scale = lax.rsqrt(jnp.mean(x * x, axis=-1, keepdims=True) + EPS)
        v = x * scale
        gate = jax.nn.sigmoid(v)
        gv = g * (gate + v * gate * (1.0 - gate))
        along = jnp.mean(gv * x, axis=-1, keepdims=True)
        out[f] = (gh[f] + scale * gv - (scale * scale * scale) * along * x).astype(BF16)


def shards(clips, lengths, w_time, w_down, cotangent):
    x = clips[0]
    cot = cotangent[0]
    frames, cells, width = x.shape
    half = frames // 2
    devices = lax.axis_size("tm")
    chips = devices // 2
    early = chips // 2
    last = len(bits_of(chips)) - 1
    taps, rows, _ = w_time.shape
    me = lax.axis_index("tm")
    lot = frames * cells

    def sds(shape, dtype=BF16):
        return jax.ShapeDtypeStruct(shape, dtype)

    def scratch(*shape):
        return pltpu.VMEM(shape, BF16)

    def call(kernel, name, inputs, outs, scratches):
        tree = (VMEM,) * len(outs) if isinstance(outs, tuple) else VMEM
        return pl.pallas_call(
            kernel,
            in_specs=[SMEM] + [VMEM] * (len(inputs) - 1),
            out_specs=tree,
            out_shape=outs,
            scratch_shapes=scratches,
            compiler_params=pltpu.CompilerParams(vmem_limit_bytes=36 * 1024 * 1024),
            cost_estimate=pl.CostEstimate(flops=1_000_000, bytes_accessed=1000, transcendentals=0),
            name=name,
        )(*inputs)

    ends = jnp.cumsum(lengths[0])
    local = me * frames + jnp.arange(-2, frames + 3, dtype=jnp.int32)
    clip = jnp.sum((ends[None, :] <= local[:, None]).astype(jnp.int32), axis=1)
    clip = jnp.where(local < 0, -1, clip)
    live_1 = (clip[2:] == clip[1:-1]).astype(jnp.int32)
    live_2 = (clip[2:] == clip[:-2]).astype(jnp.int32)
    meta = jnp.concatenate([me[None].astype(jnp.int32), live_1, live_2])

    down, time = [w_down], [w_time]
    for step in range(last):
        down = down + [exchange(part, step, "down") for part in down]
        time = time + [exchange(part, step, "time") for part in time]
    down_own = exchange(w_down, last, "down_own")
    cot_next = shifted(cot[:2], "tm", -1)
    down_late = [exchange(part, last, "down") for part in down[1:]]
    time_late = jnp.stack(time)
    first = [cot_next, down_own] + down[1:] + time[1:]
    time_late = after(time_late, cot_next, *down)
    x_before = shifted(after(x[frames - 2:], time_late), "tm", 1)
    time_late = exchange(time_late, last, "time")
    down = down + [down_own]
    down_other = [core_swap(part, "down") for part in down]
    time_other = [core_swap(part, "time") for part in time]

    h, ht = pl.pallas_call(
        functools.partial(features_kernel, chips=chips, rows=rows),
        grid=(frames,),
        in_specs=[SMEM, pl.BlockSpec((1, cells, width), lambda f: (f, 0, 0))],
        out_specs=(
            pl.BlockSpec((1, cells, width), lambda f: (f, 0, 0)),
            pl.BlockSpec((width, cells), lambda f: (0, f)),
        ),
        out_shape=(sds((frames, cells, width)), sds((width, lot))),
        scratch_shapes=[scratch(width, cells)],
        compiler_params=pltpu.CompilerParams(vmem_limit_bytes=36 * 1024 * 1024),
        cost_estimate=pl.CostEstimate(flops=FEATURES_COST, bytes_accessed=1000, transcendentals=0),
        name="features",
    )(after(meta, *first, *down_late, *down_other, *time_other), x)

    down = down + down_late + down_other + [after(core_swap(part, "down"), h) for part in down_late]

    shares = (
        sds((early, taps, rows, width), F32),
        sds((early, taps, rows, width), F32),
    ) + (sds((taps, rows, width)),) * chips
    full = scratch(taps, width, width)
    gh, gm, *time_shares = call(
        functools.partial(backward_kernel, chips=chips),
        "backward",
        [meta, cot, cot_next, ht] + down,
        (sds((frames, cells, width), F32), sds((frames + 2, cells, width))) + shares,
        [full] + [scratch((half + 1) * cells, width)] * 3 + [scratch(lot, width)] * 2,
    )

    def core_sum(shares, name, *earlier):
        low, high, *send = shares
        other = jnp.stack([after(core_swap(part, name), *earlier) for part in send]).astype(F32)
        return low + other[:early], (high + other[early:]).astype(BF16)

    def plane_step(low, other):
        total = low + other.astype(F32)
        count = total.shape[0] // 2
        return total[:count], total[count:].astype(BF16)

    def group_sum(mine, step, name):
        return mine.astype(F32) + group_exchange(mine, step, name).astype(F32)

    time_late = after(time_late, gm)
    time = time + [time_late] + time_other + [core_swap(time_late, "time")]
    low_time, high_time = core_sum(time_shares, "grad_time", x_before)
    hidden, tail, *down_shares = call(
        functools.partial(forward_kernel, chips=chips),
        "forward",
        [after(meta, high_time), x, x_before, h, cot, cot_next] + time,
        (sds((frames, cells, width)), sds((2, cells, width))) + shares,
        [full] + [scratch(lot, width)] * 2 + [scratch(width, cells)]
        + [scratch(width, half * cells)] * 2 + [scratch(half * cells, width)] * 2,
    )

    for step in range(last):
        other = after(exchange(high_time, step, "grad_time"), hidden)
        low_time, high_time = plane_step(low_time, other)
        if step == 0:
            low_down, high_down = core_sum(down_shares, "grad_down", high_time)
            cuts = [slice(i * rows // PARTS, (i + 1) * rows // PARTS) for i in range(PARTS)]
            lows = [low_down[:, :, cut] for cut in cuts]
            highs = [high_down[:, :, cut] for cut in cuts]
            grad_clips = call(
                clips_kernel,
                "clips",
                [after(meta, *highs), x, gh, gm] + time,
                sds((frames, cells, width)),
                [full] + [scratch(lot, width)] * 2,
            )
        earlier = grad_clips
        if step == last - 1:
            other = after(exchange(high_time, last, "grad_time"), grad_clips)
            mine_time = (low_time[0] + other[0].astype(F32)).astype(BF16)
            earlier = mine_time
        for i in range(PARTS):
            other = after(exchange(highs[i], step, f"grad_down{i}"), earlier)
            lows[i], highs[i] = plane_step(lows[i], other)
            earlier = highs[i]
    mine = [None] * PARTS
    for i in range(PARTS):
        other = after(exchange(highs[i], last, f"grad_down{i}"), earlier)
        mine[i] = (lows[i][0] + other[0].astype(F32)).astype(BF16)
        earlier = mine[i]
    before = shifted(after(tail, mine[TAIL]), "tm", 1)
    steps = len(bits_of(lax.axis_size("group")))
    for step in range(steps):
        if step == steps - 1:
            reduced = call(
                reduced_kernel,
                "reduced",
                [after(meta, *mine), before, hidden] + down,
                sds((half, cells, width)),
                [full] + [scratch(half * cells, width)] * 3,
            )
            earlier = reduced
        grad_time = mine_time.astype(F32) + after(group_exchange(mine_time, step, "grad_time"), earlier).astype(F32)
        if step < steps - 1:
            mine_time = grad_time.astype(BF16)
            earlier = mine_time
        else:
            earlier = grad_time
        sums = []
        for i in range(PARTS):
            other = after(group_exchange(mine[i], step, f"grad_down{i}"), earlier)
            sums.append(mine[i].astype(F32) + other.astype(F32))
            if step < steps - 1:
                mine[i] = sums[i].astype(BF16)
                earlier = mine[i]
    grad_down = jnp.concatenate(sums, axis=1)
    return reduced[None], grad_clips[None], grad_time, grad_down


def solution(mesh):
    in_specs = (
        P("group", "tm", None, None),
        P("group", None),
        P(None, "tm", None),
        P(None, "tm", None),
        P("group", "tm", None, None),
    )
    out_specs = (
        P("group", "tm", None, None),
        P("group", "tm", None, None),
        P(None, "tm", None),
        P(None, "tm", None),
    )
    return jax.shard_map(shards, mesh=mesh, in_specs=in_specs, out_specs=out_specs, check_vma=False)
```

```python
import functools

import jax
import jax.numpy as jnp
from jax import lax
from jax.experimental import pallas as pl
from jax.experimental.pallas import tpu as pltpu
from jax.sharding import PartitionSpec as P

EPS = 1e-06
PARTS = 2
TAIL = -1
FEATURES_COST = 20_000_000_000
VMEM = pl.BlockSpec(memory_space=pltpu.VMEM)
SMEM = pl.BlockSpec(memory_space=pltpu.SMEM)
F32 = jnp.float32
BF16 = jnp.bfloat16


def bits_of(count):
    bits = []
    while 1 << len(bits) < count:
        bits.append(1 << len(bits))
    return bits


def exchange(value, step, name):
    bits = bits_of(lax.axis_size("tm"))[1:]
    turn = [bits[step], bits[(step + 1) % len(bits)]]
    with jax.named_scope(f"{name}_tm_{step}"):
        route = [(i, i ^ turn[i % 2]) for i in range(lax.axis_size("tm"))]
        return lax.ppermute(value, "tm", route)


def core_swap(value, name):
    with jax.named_scope(f"{name}_tm_core"):
        return lax.ppermute(value, "tm", [(i, i ^ 1) for i in range(lax.axis_size("tm"))])


def group_exchange(value, step, name):
    groups = lax.axis_size("group")
    bits = bits_of(groups)
    turn = [bits[step], bits[(step + len(bits) // 2) % len(bits)]]
    route = [
        (t * groups + g, t * groups + (g ^ turn[t % 2]))
        for t in range(lax.axis_size("tm"))
        for g in range(groups)
    ]
    with jax.named_scope(f"{name}_group_{step}"):
        return lax.ppermute(value, ("tm", "group"), route)


def shifted(block, axis, distance):
    devices = range(lax.axis_size(axis))
    route = [(i - distance, i) for i in devices if i - distance in devices]
    with jax.named_scope(f"halo_{axis}{distance}_{block.shape[0]}"):
        return lax.ppermute(block, axis, route)


def after(value, *earlier):
    return lax.optimization_barrier((value,) + earlier)[0]


def dot(left, right):
    return jnp.dot(left, right, preferred_element_type=F32)


def dot_t(left, right):
    return lax.dot_general(left, right, (((1,), (1,)), ((), ())), preferred_element_type=F32)


def kept(flag, block):
    return jnp.where(flag > 0, block, jnp.zeros((), block.dtype))


def live(meta, tap, frame, frames):
    return meta[1 + (tap - 1) * (frames + 3) + frame]


def chip_bit(step, count, core):
    return jnp.where(core == 0, 1 << step, 1 << ((step + 1) % count))


def apart(position, chips, core, last_first):
    count = len(bits_of(chips))
    total = 0
    for step in range(count):
        place = count - 1 - step if last_first else step
        if position >> place & 1:
            total = total ^ chip_bit(step, count, core)
    return total


def block_at(meta, position, chips, rows, other, last_first):
    chip, core = meta[0] // 2, meta[0] % 2
    core = 1 - core if other else core
    block = (chip ^ apart(position, chips, core, last_first)) * 2 + core
    return pl.multiple_of(block * rows, rows)


def assemble(meta, pieces, full):
    pieces = [piece for ref in pieces for piece in ([ref.at[i] for i in range(ref.shape[0])] if len(ref.shape) == 4 else [ref])]
    taps, rows, _ = pieces[0].shape
    chips = len(pieces) // 2
    for index, source in enumerate(pieces):
        at = block_at(meta, index % chips, chips, rows, index >= chips, False)
        for tap in range(taps):
            full[tap, pl.ds(at, rows), :] = source[tap]


def place_rows(meta, chips, rows, values, target, columns):
    for index in range(2 * chips):
        at = block_at(meta, index % chips, chips, rows, index >= chips, True)
        target[index * rows:(index + 1) * rows, columns] = values[pl.ds(at, rows), :]


def split_rows(value, shares, tap):
    half, _, rows, _ = shares[0].shape
    for index in range(4 * half):
        part = value[index * rows:(index + 1) * rows]
        if index < 2 * half:
            shares[index // half][index % half, tap] = part
        else:
            shares[2 + index - 2 * half][tap] = part.astype(BF16)


def features(x):
    x = x.astype(F32)
    scale = lax.rsqrt(jnp.mean(x * x, axis=-1, keepdims=True) + EPS)
    v = x * scale
    return (v * jax.nn.sigmoid(v)).astype(BF16)


def features_kernel(meta, clips, h_out, ht_out, flip, *, chips, rows):
    cells = clips.shape[1]
    for i in range(clips.shape[0]):
        h = features(clips[i])
        h_out[i] = h
        flip[...] = h.T
        place_rows(meta, chips, rows, flip, ht_out, slice(i * cells, (i + 1) * cells))


def backward_kernel(meta, cot, cot_next, ht, *refs, chips):
    w, c0, c1, c2, m1, m2 = refs[-6:]
    *pieces, gh, gm = refs[:-8 - chips]
    shares = refs[-8 - chips:-6]
    half, cells, _ = cot.shape
    frames = 2 * half
    assemble(meta, pieces, w)

    def cot_at(j):
        return cot[j] if j < half else cot_next[j - half]

    for m in range(half + 1):
        here = slice(m * cells, (m + 1) * cells)
        c0[here] = cot_at(m)
        ahead = cot_at(m + 1)
        c1[here] = kept(live(meta, 1, 2 * m + 2, frames), ahead)
        c2[here] = kept(live(meta, 2, 2 * m + 2, frames), ahead)
    odd = dot_t(c1[...], w[1])
    for m in range(half + 1):
        here = odd[m * cells:(m + 1) * cells]
        gm[2 * m + 1] = here.astype(BF16)
        if m < half:
            gh[2 * m + 1] = here
    even = dot_t(c0[...], w[0]) + dot_t(c2[...], w[2])
    for m in range(half + 1):
        here = even[m * cells:(m + 1) * cells]
        gm[2 * m] = here.astype(BF16)
        if m < half:
            gh[2 * m] = here
    for g in range(frames):
        here = slice(g * cells, (g + 1) * cells)
        m1[here] = kept(live(meta, 1, g + 1, frames), gm[g + 1])
        m2[here] = kept(live(meta, 2, g + 2, frames), gm[g + 2])
    flat = gm[0:frames].reshape(frames * cells, gm.shape[-1])
    split_rows(dot(ht[...], flat), shares, 0)
    split_rows(dot(ht[...], m1[...]), shares, 1)
    split_rows(dot(ht[...], m2[...]), shares, 2)


def forward_kernel(meta, clips, before, h, cot, cot_next, *refs, chips):
    w, t1, t2, flip, even_t, odd_t, c1, c2 = refs[-8:]
    *pieces, hidden, tail = refs[:-10 - chips]
    shares = refs[-10 - chips:-8]
    frames, cells, width = clips.shape
    half = frames // 2
    rows = shares[0].shape[2]
    assemble(meta, pieces, w)

    h_before = [features(before[0]), features(before[1])]

    def h_at(f):
        return h[f] if f >= 0 else h_before[f + 2]

    def cot_at(j):
        return cot[j] if j < half else cot_next[j - half]

    for f in range(frames):
        here = slice(f * cells, (f + 1) * cells)
        t1[here] = kept(live(meta, 1, f, frames), h_at(f - 1))
        t2[here] = kept(live(meta, 2, f, frames), h_at(f - 2))
    for j in range(half):
        here = slice(j * cells, (j + 1) * cells)
        c1[here] = kept(live(meta, 1, 2 * j + 2, frames), cot_at(j + 1))
        c2[here] = kept(live(meta, 2, 2 * j + 2, frames), cot_at(j + 1))
    flat = h[...].reshape(frames * cells, width)
    mixed = dot(flat, w[0]) + dot(t1[...], w[1]) + dot(t2[...], w[2])
    for f in range(frames):
        value = (clips[f].astype(F32) + mixed[f * cells:(f + 1) * cells]).astype(BF16)
        hidden[f] = value
        if f >= frames - 2:
            tail[f - frames + 2] = value
        flip[...] = value.T
        columns = slice(f // 2 * cells, (f // 2 + 1) * cells)
        place_rows(meta, chips, rows, flip, odd_t if f % 2 else even_t, columns)
    flat_cot = cot[...].reshape(half * cells, width)
    split_rows(dot(even_t[...], flat_cot), shares, 0)
    split_rows(dot(odd_t[...], c1[...]), shares, 1)
    split_rows(dot(even_t[...], c2[...]), shares, 2)


def reduced_kernel(meta, before, hidden, *refs):
    *pieces, reduced, w, t0, t1, t2 = refs
    frames, cells, width = hidden.shape
    half = frames // 2
    assemble(meta, pieces, w)
    for j in range(half):
        here = slice(j * cells, (j + 1) * cells)
        t0[here] = hidden[2 * j]
        t1[here] = kept(live(meta, 1, 2 * j, frames), hidden[2 * j - 1] if j else before[1])
        t2[here] = kept(live(meta, 2, 2 * j, frames), hidden[2 * j - 2] if j else before[0])
    out = dot(t0[...], w[0]) + dot(t1[...], w[1]) + dot(t2[...], w[2])
    for j in range(half):
        reduced[j] = out[j * cells:(j + 1) * cells].astype(BF16)


def clips_kernel(meta, clips, gh, gm, *refs):
    *pieces, out, w, m1, m2 = refs
    frames, cells, width = clips.shape
    assemble(meta, pieces, w)
    for g in range(frames):
        here = slice(g * cells, (g + 1) * cells)
        m1[here] = kept(live(meta, 1, g + 1, frames), gm[g + 1])
        m2[here] = kept(live(meta, 2, g + 2, frames), gm[g + 2])
    flat = gm[0:frames].reshape(frames * cells, width)
    grad = dot_t(flat, w[0]) + dot_t(m1[...], w[1]) + dot_t(m2[...], w[2])
    for f in range(frames):
        g = grad[f * cells:(f + 1) * cells]
        x = clips[f].astype(F32)
        scale = lax.rsqrt(jnp.mean(x * x, axis=-1, keepdims=True) + EPS)
        v = x * scale
        gate = jax.nn.sigmoid(v)
        gv = g * (gate + v * gate * (1.0 - gate))
        along = jnp.mean(gv * x, axis=-1, keepdims=True)
        out[f] = (gh[f] + scale * gv - (scale * scale * scale) * along * x).astype(BF16)


def shards(clips, lengths, w_time, w_down, cotangent):
    x = clips[0]
    cot = cotangent[0]
    frames, cells, width = x.shape
    half = frames // 2
    devices = lax.axis_size("tm")
    chips = devices // 2
    early = chips // 2
    last = len(bits_of(chips)) - 1
    taps, rows, _ = w_time.shape
    me = lax.axis_index("tm")
    lot = frames * cells

    def sds(shape, dtype=BF16):
        return jax.ShapeDtypeStruct(shape, dtype)

    def scratch(*shape):
        return pltpu.VMEM(shape, BF16)

    def call(kernel, name, inputs, outs, scratches, flops=1_000_000):
        tree = (VMEM,) * len(outs) if isinstance(outs, tuple) else VMEM
        return pl.pallas_call(
            kernel,
            in_specs=[SMEM] + [VMEM] * (len(inputs) - 1),
            out_specs=tree,
            out_shape=outs,
            scratch_shapes=scratches,
            compiler_params=pltpu.CompilerParams(vmem_limit_bytes=36 * 1024 * 1024),
            cost_estimate=pl.CostEstimate(flops=flops, bytes_accessed=1000, transcendentals=0),
            name=name,
        )(*inputs)

    clips_up_to = jnp.tri(lengths.shape[1], dtype=jnp.int32)
    ends = jnp.sum(clips_up_to * lengths, axis=1)
    local = me * frames + jnp.arange(-2, frames + 3, dtype=jnp.int32)
    clip = jnp.sum((ends[None, :] <= local[:, None]).astype(jnp.int32), axis=1)
    clip = jnp.where(local < 0, -1, clip)
    live_1 = (clip[2:] == clip[1:-1]).astype(jnp.int32)
    live_2 = (clip[2:] == clip[:-2]).astype(jnp.int32)
    meta = jnp.concatenate([me[None].astype(jnp.int32), live_1, live_2])

    down, time = [w_down], [w_time]
    for step in range(last):
        down = down + [exchange(part, step, "down") for part in down]
        time = time + [exchange(part, step, "time") for part in time]
    down_own = exchange(w_down, last, "down_own")
    cot_next = shifted(cot[:2], "tm", -1)
    down_late = [exchange(part, last, "down") for part in down[1:]]
    time_late = after(jnp.pad(w_time[None], ((0, early - 1), (0, 0), (0, 0), (0, 0))), down_own)
    for i in range(1, early):
        time_late = lax.dynamic_update_slice(time_late, time[i][None], (i, 0, 0, 0))
    first = [cot_next, down_own] + down[1:] + time[1:]
    time_late = after(time_late, cot_next, *down)
    x_before = shifted(after(x[frames - 2:], time_late), "tm", 1)
    time_late = exchange(time_late, last, "time")
    down = down + [down_own]
    down_other = [core_swap(part, "down") for part in down]
    time_other = [core_swap(part, "time") for part in time]

    h, ht = call(
        functools.partial(features_kernel, chips=chips, rows=rows),
        "features",
        [after(meta, *first, *down_late, *down_other, *time_other), x],
        (sds((frames, cells, width)), sds((width, lot))),
        [scratch(width, cells)],
        FEATURES_COST,
    )

    down = down + down_late + down_other + [after(core_swap(part, "down"), h) for part in down_late]

    shares = (
        sds((early, taps, rows, width), F32),
        sds((early, taps, rows, width), F32),
    ) + (sds((taps, rows, width)),) * chips
    full = scratch(taps, width, width)
    gh, gm, *time_shares = call(
        functools.partial(backward_kernel, chips=chips),
        "backward",
        [meta, cot, cot_next, ht] + down,
        (sds((frames, cells, width), F32), sds((frames + 2, cells, width))) + shares,
        [full] + [scratch((half + 1) * cells, width)] * 3 + [scratch(lot, width)] * 2,
    )

    def core_sum(shares, name, *earlier):
        low, high, *send = shares
        other = jnp.stack([after(core_swap(part, name), *earlier) for part in send]).astype(F32)
        return low + other[:early], (high + other[early:]).astype(BF16)

    def plane_step(low, other):
        total = low + other.astype(F32)
        count = total.shape[0] // 2
        return total[:count], total[count:].astype(BF16)

    def group_sum(mine, step, name):
        return mine.astype(F32) + group_exchange(mine, step, name).astype(F32)

    time_late = after(time_late, gm)
    time = time + [time_late] + time_other + [core_swap(time_late, "time")]
    low_time, high_time = core_sum(time_shares, "grad_time", x_before)
    hidden, tail, *down_shares = call(
        functools.partial(forward_kernel, chips=chips),
        "forward",
        [after(meta, high_time), x, x_before, h, cot, cot_next] + time,
        (sds((frames, cells, width)), sds((2, cells, width))) + shares,
        [full] + [scratch(lot, width)] * 2 + [scratch(width, cells)]
        + [scratch(width, half * cells)] * 2 + [scratch(half * cells, width)] * 2,
    )

    for step in range(last):
        other = after(exchange(high_time, step, "grad_time"), hidden)
        low_time, high_time = plane_step(low_time, other)
        if step == 0:
            low_down, high_down = core_sum(down_shares, "grad_down", high_time)
            cuts = [slice(i * rows // PARTS, (i + 1) * rows // PARTS) for i in range(PARTS)]
            lows = [low_down[:, :, cut] for cut in cuts]
            highs = [high_down[:, :, cut] for cut in cuts]
            grad_clips = call(
                clips_kernel,
                "clips",
                [after(meta, *highs), x, gh, gm] + time,
                sds((frames, cells, width)),
                [full] + [scratch(lot, width)] * 2,
            )
        earlier = grad_clips
        if step == last - 1:
            other = after(exchange(high_time, last, "grad_time"), grad_clips)
            mine_time = (low_time[0] + other[0].astype(F32)).astype(BF16)
            earlier = mine_time
        for i in range(PARTS):
            other = after(exchange(highs[i], step, f"grad_down{i}"), earlier)
            lows[i], highs[i] = plane_step(lows[i], other)
            earlier = highs[i]
    mine = [None] * PARTS
    for i in range(PARTS):
        other = after(exchange(highs[i], last, f"grad_down{i}"), earlier)
        mine[i] = (lows[i][0] + other[0].astype(F32)).astype(BF16)
        earlier = mine[i]
    before = shifted(after(tail, mine[TAIL]), "tm", 1)
    steps = len(bits_of(lax.axis_size("group")))
    for step in range(steps):
        if step == steps - 1:
            reduced = call(
                reduced_kernel,
                "reduced",
                [after(meta, *mine), before, hidden] + down,
                sds((half, cells, width)),
                [full] + [scratch(half * cells, width)] * 3,
            )
            earlier = reduced
        grad_time = mine_time.astype(F32) + after(group_exchange(mine_time, step, "grad_time"), earlier).astype(F32)
        if step < steps - 1:
            mine_time = grad_time.astype(BF16)
            earlier = mine_time
        else:
            earlier = grad_time
        sums = []
        for i in range(PARTS):
            other = after(group_exchange(mine[i], step, f"grad_down{i}"), earlier)
            sums.append(mine[i].astype(F32) + other.astype(F32))
            if step < steps - 1:
                mine[i] = sums[i].astype(BF16)
                earlier = mine[i]
    grad_down = jnp.concatenate(sums, axis=1)
    return reduced[None], grad_clips[None], grad_time, grad_down


def solution(mesh):
    in_specs = (
        P("group", "tm", None, None),
        P("group", None),
        P(None, "tm", None),
        P(None, "tm", None),
        P("group", "tm", None, None),
    )
    out_specs = (
        P("group", "tm", None, None),
        P("group", "tm", None, None),
        P(None, "tm", None),
        P(None, "tm", None),
    )
    return jax.shard_map(shards, mesh=mesh, in_specs=in_specs, out_specs=out_specs, check_vma=False)
```

```python
import functools

import jax
import jax.numpy as jnp
from jax import lax
from jax.experimental import pallas as pl
from jax.experimental.pallas import tpu as pltpu
from jax.sharding import PartitionSpec as P

EPS = 1e-06
PARTS = 2
TAIL = -1
FEATURES_COST = 20_000_000_000
VMEM = pl.BlockSpec(memory_space=pltpu.VMEM)
SMEM = pl.BlockSpec(memory_space=pltpu.SMEM)
F32 = jnp.float32
BF16 = jnp.bfloat16


def bits_of(count):
    bits = []
    while 1 << len(bits) < count:
        bits.append(1 << len(bits))
    return bits


def exchange(value, step, name):
    bits = bits_of(lax.axis_size("tm"))[1:]
    turn = [bits[step], bits[(step + 1) % len(bits)]]
    with jax.named_scope(f"{name}_tm_{step}"):
        route = [(i, i ^ turn[i % 2]) for i in range(lax.axis_size("tm"))]
        return lax.ppermute(value, "tm", route)


def core_swap(value, name):
    with jax.named_scope(f"{name}_tm_core"):
        return lax.ppermute(value, "tm", [(i, i ^ 1) for i in range(lax.axis_size("tm"))])


def group_exchange(value, step, name):
    groups = lax.axis_size("group")
    bits = bits_of(groups)
    turn = [bits[step], bits[(step + len(bits) // 2) % len(bits)]]
    route = [
        (t * groups + g, t * groups + (g ^ turn[t % 2]))
        for t in range(lax.axis_size("tm"))
        for g in range(groups)
    ]
    with jax.named_scope(f"{name}_group_{step}"):
        return lax.ppermute(value, ("tm", "group"), route)


def shifted(block, axis, distance):
    devices = range(lax.axis_size(axis))
    route = [(i - distance, i) for i in devices if i - distance in devices]
    with jax.named_scope(f"halo_{axis}{distance}_{block.shape[0]}"):
        return lax.ppermute(block, axis, route)


def after(value, *earlier):
    return lax.optimization_barrier((value,) + earlier)[0]


def dot(left, right):
    return jnp.dot(left, right, preferred_element_type=F32)


def dot_t(left, right):
    return lax.dot_general(left, right, (((1,), (1,)), ((), ())), preferred_element_type=F32)


def kept(flag, block):
    return jnp.where(flag > 0, block, jnp.zeros((), block.dtype))


def live(meta, tap, frame, frames):
    return meta[1 + (tap - 1) * (frames + 3) + frame]


def chip_bit(step, count, core):
    return jnp.where(core == 0, 1 << step, 1 << ((step + 1) % count))


def apart(position, chips, core, last_first):
    count = len(bits_of(chips))
    total = 0
    for step in range(count):
        place = count - 1 - step if last_first else step
        if position >> place & 1:
            total = total ^ chip_bit(step, count, core)
    return total


def block_at(meta, position, chips, rows, other, last_first):
    chip, core = meta[0] // 2, meta[0] % 2
    core = 1 - core if other else core
    block = (chip ^ apart(position, chips, core, last_first)) * 2 + core
    return pl.multiple_of(block * rows, rows)


def assemble(meta, pieces, full):
    pieces = [piece for ref in pieces for piece in ([ref.at[i] for i in range(ref.shape[0])] if len(ref.shape) == 4 else [ref])]
    taps, rows, _ = pieces[0].shape
    chips = len(pieces) // 2
    for index, source in enumerate(pieces):
        at = block_at(meta, index % chips, chips, rows, index >= chips, False)
        for tap in range(taps):
            full[tap, pl.ds(at, rows), :] = source[tap]


def place_rows(meta, chips, rows, values, target, columns):
    for index in range(2 * chips):
        at = block_at(meta, index % chips, chips, rows, index >= chips, True)
        target[index * rows:(index + 1) * rows, columns] = values[pl.ds(at, rows), :]


def split_rows(value, shares, tap):
    half, _, rows, _ = shares[0].shape
    for index in range(4 * half):
        part = value[index * rows:(index + 1) * rows]
        if index < 2 * half:
            shares[index // half][index % half, tap] = part
        else:
            shares[2 + index - 2 * half][tap] = part.astype(BF16)


def features(x):
    x = x.astype(F32)
    scale = lax.rsqrt(jnp.mean(x * x, axis=-1, keepdims=True) + EPS)
    v = x * scale
    return (v * jax.nn.sigmoid(v)).astype(BF16)


def features_kernel(meta, clips, h_out, ht_out, flip, *, chips, rows):
    cells = clips.shape[1]
    for i in range(clips.shape[0]):
        h = features(clips[i])
        h_out[i] = h
        flip[...] = h.T
        place_rows(meta, chips, rows, flip, ht_out, slice(i * cells, (i + 1) * cells))


def backward_kernel(meta, cot, cot_next, ht, *refs, chips):
    w, c0, c1, c2, m1, m2 = refs[-6:]
    *pieces, gh, gm = refs[:-8 - chips]
    shares = refs[-8 - chips:-6]
    half, cells, _ = cot.shape
    frames = 2 * half
    assemble(meta, pieces, w)

    def cot_at(j):
        return cot[j] if j < half else cot_next[j - half]

    for m in range(half + 1):
        here = slice(m * cells, (m + 1) * cells)
        c0[here] = cot_at(m)
        ahead = cot_at(m + 1)
        c1[here] = kept(live(meta, 1, 2 * m + 2, frames), ahead)
        c2[here] = kept(live(meta, 2, 2 * m + 2, frames), ahead)
    odd = dot_t(c1[...], w[1])
    for m in range(half + 1):
        here = odd[m * cells:(m + 1) * cells]
        gm[2 * m + 1] = here.astype(BF16)
        if m < half:
            gh[2 * m + 1] = here
    even = dot_t(c0[...], w[0]) + dot_t(c2[...], w[2])
    for m in range(half + 1):
        here = even[m * cells:(m + 1) * cells]
        gm[2 * m] = here.astype(BF16)
        if m < half:
            gh[2 * m] = here
    for g in range(frames):
        here = slice(g * cells, (g + 1) * cells)
        m1[here] = kept(live(meta, 1, g + 1, frames), gm[g + 1])
        m2[here] = kept(live(meta, 2, g + 2, frames), gm[g + 2])
    flat = gm[0:frames].reshape(frames * cells, gm.shape[-1])
    split_rows(dot(ht[...], flat), shares, 0)
    split_rows(dot(ht[...], m1[...]), shares, 1)
    split_rows(dot(ht[...], m2[...]), shares, 2)


def forward_kernel(meta, clips, before, h, cot, cot_next, *refs, chips):
    w, t1, t2, flip, even_t, odd_t, c1, c2 = refs[-8:]
    *pieces, hidden, tail = refs[:-10 - chips]
    shares = refs[-10 - chips:-8]
    frames, cells, width = clips.shape
    half = frames // 2
    rows = shares[0].shape[2]
    assemble(meta, pieces, w)

    h_before = [features(before[0]), features(before[1])]

    def h_at(f):
        return h[f] if f >= 0 else h_before[f + 2]

    def cot_at(j):
        return cot[j] if j < half else cot_next[j - half]

    for f in range(frames):
        here = slice(f * cells, (f + 1) * cells)
        t1[here] = kept(live(meta, 1, f, frames), h_at(f - 1))
        t2[here] = kept(live(meta, 2, f, frames), h_at(f - 2))
    for j in range(half):
        here = slice(j * cells, (j + 1) * cells)
        c1[here] = kept(live(meta, 1, 2 * j + 2, frames), cot_at(j + 1))
        c2[here] = kept(live(meta, 2, 2 * j + 2, frames), cot_at(j + 1))
    flat = h[...].reshape(frames * cells, width)
    mixed = dot(flat, w[0]) + dot(t1[...], w[1]) + dot(t2[...], w[2])
    for f in range(frames):
        value = (clips[f].astype(F32) + mixed[f * cells:(f + 1) * cells]).astype(BF16)
        hidden[f] = value
        if f >= frames - 2:
            tail[f - frames + 2] = value
        flip[...] = value.T
        columns = slice(f // 2 * cells, (f // 2 + 1) * cells)
        place_rows(meta, chips, rows, flip, odd_t if f % 2 else even_t, columns)
    flat_cot = cot[...].reshape(half * cells, width)
    split_rows(dot(even_t[...], flat_cot), shares, 0)
    split_rows(dot(odd_t[...], c1[...]), shares, 1)
    split_rows(dot(even_t[...], c2[...]), shares, 2)


def reduced_kernel(meta, before, hidden, *refs):
    *pieces, reduced, w, t0, t1, t2 = refs
    frames, cells, width = hidden.shape
    half = frames // 2
    assemble(meta, pieces, w)
    for j in range(half):
        here = slice(j * cells, (j + 1) * cells)
        t0[here] = hidden[2 * j]
        t1[here] = kept(live(meta, 1, 2 * j, frames), hidden[2 * j - 1] if j else before[1])
        t2[here] = kept(live(meta, 2, 2 * j, frames), hidden[2 * j - 2] if j else before[0])
    out = dot(t0[...], w[0]) + dot(t1[...], w[1]) + dot(t2[...], w[2])
    for j in range(half):
        reduced[j] = out[j * cells:(j + 1) * cells].astype(BF16)


def clips_kernel(meta, clips, gh, gm, *refs):
    *pieces, out, w, m1, m2 = refs
    frames, cells, width = clips.shape
    assemble(meta, pieces, w)
    for g in range(frames):
        here = slice(g * cells, (g + 1) * cells)
        m1[here] = kept(live(meta, 1, g + 1, frames), gm[g + 1])
        m2[here] = kept(live(meta, 2, g + 2, frames), gm[g + 2])
    flat = gm[0:frames].reshape(frames * cells, width)
    grad = dot_t(flat, w[0]) + dot_t(m1[...], w[1]) + dot_t(m2[...], w[2])
    for f in range(frames):
        g = grad[f * cells:(f + 1) * cells]
        x = clips[f].astype(F32)
        scale = lax.rsqrt(jnp.mean(x * x, axis=-1, keepdims=True) + EPS)
        v = x * scale
        gate = jax.nn.sigmoid(v)
        gv = g * (gate + v * gate * (1.0 - gate))
        along = jnp.mean(gv * x, axis=-1, keepdims=True)
        out[f] = (gh[f] + scale * gv - (scale * scale * scale) * along * x).astype(BF16)


def shards(clips, lengths, w_time, w_down, cotangent):
    x = clips[0]
    cot = cotangent[0]
    frames, cells, width = x.shape
    half = frames // 2
    devices = lax.axis_size("tm")
    chips = devices // 2
    early = chips // 2
    last = len(bits_of(chips)) - 1
    taps, rows, _ = w_time.shape
    me = lax.axis_index("tm")
    lot = frames * cells

    def sds(shape, dtype=BF16):
        return jax.ShapeDtypeStruct(shape, dtype)

    def scratch(*shape):
        return pltpu.VMEM(shape, BF16)

    def call(kernel, name, inputs, outs, scratches, flops=1_000_000):
        tree = (VMEM,) * len(outs) if isinstance(outs, tuple) else VMEM
        return pl.pallas_call(
            kernel,
            in_specs=[SMEM] + [VMEM] * (len(inputs) - 1),
            out_specs=tree,
            out_shape=outs,
            scratch_shapes=scratches,
            compiler_params=pltpu.CompilerParams(vmem_limit_bytes=36 * 1024 * 1024),
            cost_estimate=pl.CostEstimate(flops=flops, bytes_accessed=1000, transcendentals=0),
            name=name,
        )(*inputs)

    clips_up_to = jnp.tri(lengths.shape[1], dtype=jnp.int32)
    ends = jnp.sum(clips_up_to * lengths, axis=1)
    local = me * frames + jnp.arange(-2, frames + 3, dtype=jnp.int32)
    clip = jnp.sum((ends[None, :] <= local[:, None]).astype(jnp.int32), axis=1)
    clip = jnp.where(local < 0, -1, clip)
    live_1 = (clip[2:] == clip[1:-1]).astype(jnp.int32)
    live_2 = (clip[2:] == clip[:-2]).astype(jnp.int32)
    meta = jnp.concatenate([me[None].astype(jnp.int32), live_1, live_2])

    down, time = [w_down], [w_time]
    for step in range(last):
        down = down + [exchange(part, step, "down") for part in down]
        time = time + [exchange(part, step, "time") for part in time]
    down_own = exchange(w_down, last, "down_own")
    cot_next = shifted(cot[:2], "tm", -1)
    down_late = [exchange(part, last, "down") for part in down[1:]]
    time_late = after(jnp.pad(w_time[None], ((0, early - 1), (0, 0), (0, 0), (0, 0))), down_own)
    for i in range(1, early):
        time_late = lax.dynamic_update_slice(time_late, time[i][None], (i, 0, 0, 0))
    first = [cot_next, down_own] + down[1:] + time[1:]
    time_late = after(time_late, cot_next, *down)
    x_before = shifted(after(x[frames - 2:], time_late), "tm", 1)
    time_late = exchange(time_late, last, "time")
    down = down + [down_own]
    down_other = [core_swap(part, "down") for part in down]
    time_other = [core_swap(part, "time") for part in time]

    h, ht = call(
        functools.partial(features_kernel, chips=chips, rows=rows),
        "features",
        [after(me[None].astype(jnp.int32), *first, *down_late, *down_other, *time_other), x],
        (sds((frames, cells, width)), sds((width, lot))),
        [scratch(width, cells)],
        FEATURES_COST,
    )

    down = down + down_late + down_other + [after(core_swap(part, "down"), h) for part in down_late]

    shares = (
        sds((early, taps, rows, width), F32),
        sds((early, taps, rows, width), F32),
    ) + (sds((taps, rows, width)),) * chips
    full = scratch(taps, width, width)
    gh, gm, *time_shares = call(
        functools.partial(backward_kernel, chips=chips),
        "backward",
        [meta, cot, cot_next, ht] + down,
        (sds((frames, cells, width), F32), sds((frames + 2, cells, width))) + shares,
        [full] + [scratch((half + 1) * cells, width)] * 3 + [scratch(lot, width)] * 2,
    )

    def core_sum(shares, name, *earlier):
        low, high, *send = shares
        other = jnp.stack([after(core_swap(part, name), *earlier) for part in send]).astype(F32)
        return low + other[:early], (high + other[early:]).astype(BF16)

    def plane_step(low, other):
        total = low + other.astype(F32)
        count = total.shape[0] // 2
        return total[:count], total[count:].astype(BF16)

    def group_sum(mine, step, name):
        return mine.astype(F32) + group_exchange(mine, step, name).astype(F32)

    time_late = after(time_late, gm)
    time = time + [time_late] + time_other + [core_swap(time_late, "time")]
    low_time, high_time = core_sum(time_shares, "grad_time", x_before)
    hidden, tail, *down_shares = call(
        functools.partial(forward_kernel, chips=chips),
        "forward",
        [after(meta, high_time), x, x_before, h, cot, cot_next] + time,
        (sds((frames, cells, width)), sds((2, cells, width))) + shares,
        [full] + [scratch(lot, width)] * 2 + [scratch(width, cells)]
        + [scratch(width, half * cells)] * 2 + [scratch(half * cells, width)] * 2,
    )

    for step in range(last):
        other = after(exchange(high_time, step, "grad_time"), hidden)
        low_time, high_time = plane_step(low_time, other)
        if step == 0:
            low_down, high_down = core_sum(down_shares, "grad_down", high_time)
            cuts = [slice(i * rows // PARTS, (i + 1) * rows // PARTS) for i in range(PARTS)]
            lows = [low_down[:, :, cut] for cut in cuts]
            highs = [high_down[:, :, cut] for cut in cuts]
            grad_clips = call(
                clips_kernel,
                "clips",
                [after(meta, *highs), x, gh, gm] + time,
                sds((frames, cells, width)),
                [full] + [scratch(lot, width)] * 2,
            )
        earlier = grad_clips
        if step == last - 1:
            other = after(exchange(high_time, last, "grad_time"), grad_clips)
            mine_time = (low_time[0] + other[0].astype(F32)).astype(BF16)
            earlier = mine_time
        for i in range(PARTS):
            other = after(exchange(highs[i], step, f"grad_down{i}"), earlier)
            lows[i], highs[i] = plane_step(lows[i], other)
            earlier = highs[i]
    mine = [None] * PARTS
    for i in range(PARTS):
        other = after(exchange(highs[i], last, f"grad_down{i}"), earlier)
        mine[i] = (lows[i][0] + other[0].astype(F32)).astype(BF16)
        earlier = mine[i]
    before = shifted(after(tail, mine[TAIL]), "tm", 1)
    steps = len(bits_of(lax.axis_size("group")))
    for step in range(steps):
        if step == steps - 1:
            reduced = call(
                reduced_kernel,
                "reduced",
                [after(meta, *mine), before, hidden] + down,
                sds((half, cells, width)),
                [full] + [scratch(half * cells, width)] * 3,
            )
            earlier = reduced
        grad_time = mine_time.astype(F32) + after(group_exchange(mine_time, step, "grad_time"), earlier).astype(F32)
        if step < steps - 1:
            mine_time = grad_time.astype(BF16)
            earlier = mine_time
        else:
            earlier = grad_time
        sums = []
        for i in range(PARTS):
            other = after(group_exchange(mine[i], step, f"grad_down{i}"), earlier)
            sums.append(mine[i].astype(F32) + other.astype(F32))
            if step < steps - 1:
                mine[i] = sums[i].astype(BF16)
                earlier = mine[i]
    grad_down = jnp.concatenate(sums, axis=1)
    return reduced[None], grad_clips[None], grad_time, grad_down


def solution(mesh):
    in_specs = (
        P("group", "tm", None, None),
        P("group", None),
        P(None, "tm", None),
        P(None, "tm", None),
        P("group", "tm", None, None),
    )
    out_specs = (
        P("group", "tm", None, None),
        P("group", "tm", None, None),
        P(None, "tm", None),
        P(None, "tm", None),
    )
    return jax.shard_map(shards, mesh=mesh, in_specs=in_specs, out_specs=out_specs, check_vma=False)
```

```python
import functools

import jax
import jax.numpy as jnp
from jax import lax
from jax.experimental import pallas as pl
from jax.experimental.pallas import tpu as pltpu
from jax.sharding import PartitionSpec as P

EPS = 1e-06
PARTS = 2
TAIL = -1
FEATURES_COST = 20_000_000_000
VMEM = pl.BlockSpec(memory_space=pltpu.VMEM)
SMEM = pl.BlockSpec(memory_space=pltpu.SMEM)
F32 = jnp.float32
BF16 = jnp.bfloat16


def bits_of(count):
    bits = []
    while 1 << len(bits) < count:
        bits.append(1 << len(bits))
    return bits


def exchange(value, step, name):
    bits = bits_of(lax.axis_size("tm"))[1:]
    turn = [bits[step], bits[(step + 1) % len(bits)]]
    with jax.named_scope(f"{name}_tm_{step}"):
        route = [(i, i ^ turn[i % 2]) for i in range(lax.axis_size("tm"))]
        return lax.ppermute(value, "tm", route)


def core_swap(value, name):
    with jax.named_scope(f"{name}_tm_core"):
        return lax.ppermute(value, "tm", [(i, i ^ 1) for i in range(lax.axis_size("tm"))])


def group_exchange(value, step, name):
    groups = lax.axis_size("group")
    bits = bits_of(groups)
    turn = [bits[step], bits[(step + len(bits) // 2) % len(bits)]]
    route = [
        (t * groups + g, t * groups + (g ^ turn[t % 2]))
        for t in range(lax.axis_size("tm"))
        for g in range(groups)
    ]
    with jax.named_scope(f"{name}_group_{step}"):
        return lax.ppermute(value, ("tm", "group"), route)


def shifted(block, axis, distance):
    devices = range(lax.axis_size(axis))
    route = [(i - distance, i) for i in devices if i - distance in devices]
    with jax.named_scope(f"halo_{axis}{distance}_{block.shape[0]}"):
        return lax.ppermute(block, axis, route)


def after(value, *earlier):
    return lax.optimization_barrier((value,) + earlier)[0]


def dot(left, right):
    return jnp.dot(left, right, preferred_element_type=F32)


def dot_t(left, right):
    return lax.dot_general(left, right, (((1,), (1,)), ((), ())), preferred_element_type=F32)


def kept(flag, block):
    return jnp.where(flag > 0, block, jnp.zeros((), block.dtype))


def live(meta, tap, frame, frames):
    return meta[1 + (tap - 1) * (frames + 3) + frame]


def chip_bit(step, count, core):
    return jnp.where(core == 0, 1 << step, 1 << ((step + 1) % count))


def apart(position, chips, core, last_first):
    count = len(bits_of(chips))
    total = 0
    for step in range(count):
        place = count - 1 - step if last_first else step
        if position >> place & 1:
            total = total ^ chip_bit(step, count, core)
    return total


def block_at(meta, position, chips, rows, other, last_first):
    chip, core = meta[0] // 2, meta[0] % 2
    core = 1 - core if other else core
    block = (chip ^ apart(position, chips, core, last_first)) * 2 + core
    return pl.multiple_of(block * rows, rows)


def assemble(meta, pieces, full):
    pieces = [piece for ref in pieces for piece in ([ref.at[i] for i in range(ref.shape[0])] if len(ref.shape) == 4 else [ref])]
    taps, rows, _ = pieces[0].shape
    chips = len(pieces) // 2
    for index, source in enumerate(pieces):
        at = block_at(meta, index % chips, chips, rows, index >= chips, False)
        for tap in range(taps):
            full[tap, pl.ds(at, rows), :] = source[tap]


def place_rows(meta, chips, rows, values, target, columns):
    for index in range(2 * chips):
        at = block_at(meta, index % chips, chips, rows, index >= chips, True)
        target[index * rows:(index + 1) * rows, columns] = values[pl.ds(at, rows), :]


def split_rows(value, shares, tap):
    half, _, rows, _ = shares[0].shape
    for index in range(4 * half):
        part = value[index * rows:(index + 1) * rows]
        if index < 2 * half:
            shares[index // half][index % half, tap] = part
        else:
            shares[2 + index - 2 * half][tap] = part.astype(BF16)


def features(x):
    x = x.astype(F32)
    scale = lax.rsqrt(jnp.mean(x * x, axis=-1, keepdims=True) + EPS)
    v = x * scale
    return (v * jax.nn.sigmoid(v)).astype(BF16)


def features_kernel(meta, clips, h_out, ht_out, flip, *, chips, rows):
    cells = clips.shape[1]
    for i in range(clips.shape[0]):
        h = features(clips[i])
        h_out[i] = h
        flip[...] = h.T
        place_rows(meta, chips, rows, flip, ht_out, slice(i * cells, (i + 1) * cells))


def backward_kernel(meta, cot, cot_next, ht, *refs, chips):
    w, c0, c1, c2, m1, m2 = refs[-6:]
    *pieces, gh, gm = refs[:-8 - chips]
    shares = refs[-8 - chips:-6]
    half, cells, _ = cot.shape
    frames = 2 * half
    assemble(meta, pieces, w)

    def cot_at(j):
        return cot[j] if j < half else cot_next[j - half]

    for m in range(half + 1):
        here = slice(m * cells, (m + 1) * cells)
        c0[here] = cot_at(m)
        ahead = cot_at(m + 1)
        c1[here] = kept(live(meta, 1, 2 * m + 2, frames), ahead)
        c2[here] = kept(live(meta, 2, 2 * m + 2, frames), ahead)
    odd = dot_t(c1[...], w[1])
    for m in range(half + 1):
        here = odd[m * cells:(m + 1) * cells]
        gm[2 * m + 1] = here.astype(BF16)
        if m < half:
            gh[2 * m + 1] = here
    even = dot_t(c0[...], w[0]) + dot_t(c2[...], w[2])
    for m in range(half + 1):
        here = even[m * cells:(m + 1) * cells]
        gm[2 * m] = here.astype(BF16)
        if m < half:
            gh[2 * m] = here
    for g in range(frames):
        here = slice(g * cells, (g + 1) * cells)
        m1[here] = kept(live(meta, 1, g + 1, frames), gm[g + 1])
        m2[here] = kept(live(meta, 2, g + 2, frames), gm[g + 2])
    flat = gm[0:frames].reshape(frames * cells, gm.shape[-1])
    split_rows(dot(ht[...], flat), shares, 0)
    split_rows(dot(ht[...], m1[...]), shares, 1)
    split_rows(dot(ht[...], m2[...]), shares, 2)


def forward_kernel(meta, clips, before, h, cot, cot_next, *refs, chips):
    w, t1, t2, flip, even_t, odd_t, c1, c2 = refs[-8:]
    *pieces, hidden, tail = refs[:-10 - chips]
    shares = refs[-10 - chips:-8]
    frames, cells, width = clips.shape
    half = frames // 2
    rows = shares[0].shape[2]
    assemble(meta, pieces, w)

    h_before = [features(before[0]), features(before[1])]

    def h_at(f):
        return h[f] if f >= 0 else h_before[f + 2]

    def cot_at(j):
        return cot[j] if j < half else cot_next[j - half]

    for f in range(frames):
        here = slice(f * cells, (f + 1) * cells)
        t1[here] = kept(live(meta, 1, f, frames), h_at(f - 1))
        t2[here] = kept(live(meta, 2, f, frames), h_at(f - 2))
    for j in range(half):
        here = slice(j * cells, (j + 1) * cells)
        c1[here] = kept(live(meta, 1, 2 * j + 2, frames), cot_at(j + 1))
        c2[here] = kept(live(meta, 2, 2 * j + 2, frames), cot_at(j + 1))
    flat = h[...].reshape(frames * cells, width)
    mixed = dot(flat, w[0]) + dot(t1[...], w[1]) + dot(t2[...], w[2])
    for f in range(frames):
        value = (clips[f].astype(F32) + mixed[f * cells:(f + 1) * cells]).astype(BF16)
        hidden[f] = value
        if f >= frames - 2:
            tail[f - frames + 2] = value
        flip[...] = value.T
        columns = slice(f // 2 * cells, (f // 2 + 1) * cells)
        place_rows(meta, chips, rows, flip, odd_t if f % 2 else even_t, columns)
    flat_cot = cot[...].reshape(half * cells, width)
    split_rows(dot(even_t[...], flat_cot), shares, 0)
    split_rows(dot(odd_t[...], c1[...]), shares, 1)
    split_rows(dot(even_t[...], c2[...]), shares, 2)


def reduced_kernel(meta, before, hidden, *refs):
    *pieces, reduced, w, t0, t1, t2 = refs
    frames, cells, width = hidden.shape
    half = frames // 2
    assemble(meta, pieces, w)
    for j in range(half):
        here = slice(j * cells, (j + 1) * cells)
        t0[here] = hidden[2 * j]
        t1[here] = kept(live(meta, 1, 2 * j, frames), hidden[2 * j - 1] if j else before[1])
        t2[here] = kept(live(meta, 2, 2 * j, frames), hidden[2 * j - 2] if j else before[0])
    out = dot(t0[...], w[0]) + dot(t1[...], w[1]) + dot(t2[...], w[2])
    for j in range(half):
        reduced[j] = out[j * cells:(j + 1) * cells].astype(BF16)


def clips_kernel(meta, clips, gh, gm, *refs):
    *pieces, out, w, m1, m2 = refs
    frames, cells, width = clips.shape
    assemble(meta, pieces, w)
    for g in range(frames):
        here = slice(g * cells, (g + 1) * cells)
        m1[here] = kept(live(meta, 1, g + 1, frames), gm[g + 1])
        m2[here] = kept(live(meta, 2, g + 2, frames), gm[g + 2])
    flat = gm[0:frames].reshape(frames * cells, width)
    grad = dot_t(flat, w[0]) + dot_t(m1[...], w[1]) + dot_t(m2[...], w[2])
    for f in range(frames):
        g = grad[f * cells:(f + 1) * cells]
        x = clips[f].astype(F32)
        scale = lax.rsqrt(jnp.mean(x * x, axis=-1, keepdims=True) + EPS)
        v = x * scale
        gate = jax.nn.sigmoid(v)
        gv = g * (gate + v * gate * (1.0 - gate))
        along = jnp.mean(gv * x, axis=-1, keepdims=True)
        out[f] = (gh[f] + scale * gv - (scale * scale * scale) * along * x).astype(BF16)


def shards(clips, lengths, w_time, w_down, cotangent):
    x = clips[0]
    cot = cotangent[0]
    frames, cells, width = x.shape
    half = frames // 2
    devices = lax.axis_size("tm")
    chips = devices // 2
    early = chips // 2
    last = len(bits_of(chips)) - 1
    taps, rows, _ = w_time.shape
    me = lax.axis_index("tm")
    lot = frames * cells

    def sds(shape, dtype=BF16):
        return jax.ShapeDtypeStruct(shape, dtype)

    def scratch(*shape):
        return pltpu.VMEM(shape, BF16)

    def call(kernel, name, inputs, outs, scratches, flops=1_000_000):
        tree = (VMEM,) * len(outs) if isinstance(outs, tuple) else VMEM
        return pl.pallas_call(
            kernel,
            in_specs=[SMEM] + [VMEM] * (len(inputs) - 1),
            out_specs=tree,
            out_shape=outs,
            scratch_shapes=scratches,
            compiler_params=pltpu.CompilerParams(vmem_limit_bytes=36 * 1024 * 1024),
            cost_estimate=pl.CostEstimate(flops=flops, bytes_accessed=1000, transcendentals=0),
            name=name,
        )(*inputs)

    clips_up_to = jnp.tri(lengths.shape[1], dtype=jnp.int32)
    ends = jnp.sum(clips_up_to * lengths, axis=1)
    local = me * frames + jnp.arange(-2, frames + 3, dtype=jnp.int32)
    clip = jnp.sum((ends[None, :] <= local[:, None]).astype(jnp.int32), axis=1)
    clip = jnp.where(local < 0, -1, clip)
    live_1 = (clip[2:] == clip[1:-1]).astype(jnp.int32)
    live_2 = (clip[2:] == clip[:-2]).astype(jnp.int32)
    meta = jnp.concatenate([me[None].astype(jnp.int32), live_1, live_2])

    down, time = [w_down], [w_time]
    for step in range(last):
        down = down + [exchange(part, step, "down") for part in down]
        time = time + [exchange(part, step, "time") for part in time]
    down_own = exchange(w_down, last, "down_own")
    rims = lax.optimization_barrier(jnp.concatenate([cot[:2], x[frames - 2:]]))
    cot_next = shifted(rims[:2], "tm", -1)
    down_late = [exchange(part, last, "down") for part in down[1:]]
    time_late = after(jnp.pad(w_time[None], ((0, early - 1), (0, 0), (0, 0), (0, 0))), down_own)
    for i in range(1, early):
        time_late = lax.dynamic_update_slice(time_late, time[i][None], (i, 0, 0, 0))
    first = [cot_next, down_own] + down[1:] + time[1:]
    time_late = after(time_late, cot_next, *down)
    x_before = shifted(after(rims[2:], time_late), "tm", 1)
    time_late = exchange(time_late, last, "time")
    down = down + [down_own]
    down_other = [core_swap(part, "down") for part in down]
    time_other = [core_swap(part, "time") for part in time]

    h, ht = call(
        functools.partial(features_kernel, chips=chips, rows=rows),
        "features",
        [after(me[None].astype(jnp.int32), *first, *down_late, *down_other, *time_other), x],
        (sds((frames, cells, width)), sds((width, lot))),
        [scratch(width, cells)],
        FEATURES_COST,
    )

    down = down + down_late + down_other + [after(core_swap(part, "down"), h) for part in down_late]

    shares = (
        sds((early, taps, rows, width), F32),
        sds((early, taps, rows, width), F32),
    ) + (sds((taps, rows, width)),) * chips
    full = scratch(taps, width, width)
    gh, gm, *time_shares = call(
        functools.partial(backward_kernel, chips=chips),
        "backward",
        [meta, cot, cot_next, ht] + down,
        (sds((frames, cells, width), F32), sds((frames + 2, cells, width))) + shares,
        [full] + [scratch((half + 1) * cells, width)] * 3 + [scratch(lot, width)] * 2,
    )

    def core_sum(shares, name, *earlier):
        low, high, *send = shares
        other = jnp.stack([after(core_swap(part, name), *earlier) for part in send]).astype(F32)
        return low + other[:early], (high + other[early:]).astype(BF16)

    def plane_step(low, other):
        total = low + other.astype(F32)
        count = total.shape[0] // 2
        return total[:count], total[count:].astype(BF16)

    def group_sum(mine, step, name):
        return mine.astype(F32) + group_exchange(mine, step, name).astype(F32)

    time_late = after(time_late, gm)
    time = time + [time_late] + time_other + [core_swap(time_late, "time")]
    low_time, high_time = core_sum(time_shares, "grad_time", x_before)
    hidden, tail, *down_shares = call(
        functools.partial(forward_kernel, chips=chips),
        "forward",
        [after(meta, high_time), x, x_before, h, cot, cot_next] + time,
        (sds((frames, cells, width)), sds((2, cells, width))) + shares,
        [full] + [scratch(lot, width)] * 2 + [scratch(width, cells)]
        + [scratch(width, half * cells)] * 2 + [scratch(half * cells, width)] * 2,
    )

    for step in range(last):
        other = after(exchange(high_time, step, "grad_time"), hidden)
        low_time, high_time = plane_step(low_time, other)
        if step == 0:
            low_down, high_down = core_sum(down_shares, "grad_down", high_time)
            cuts = [slice(i * rows // PARTS, (i + 1) * rows // PARTS) for i in range(PARTS)]
            lows = [low_down[:, :, cut] for cut in cuts]
            highs = [high_down[:, :, cut] for cut in cuts]
            grad_clips = call(
                clips_kernel,
                "clips",
                [after(meta, *highs), x, gh, gm] + time,
                sds((frames, cells, width)),
                [full] + [scratch(lot, width)] * 2,
            )
        earlier = grad_clips
        if step == last - 1:
            other = after(exchange(high_time, last, "grad_time"), grad_clips)
            mine_time = (low_time[0] + other[0].astype(F32)).astype(BF16)
            earlier = mine_time
        for i in range(PARTS):
            other = after(exchange(highs[i], step, f"grad_down{i}"), earlier)
            lows[i], highs[i] = plane_step(lows[i], other)
            earlier = highs[i]
    mine = [None] * PARTS
    for i in range(PARTS):
        other = after(exchange(highs[i], last, f"grad_down{i}"), earlier)
        mine[i] = (lows[i][0] + other[0].astype(F32)).astype(BF16)
        earlier = mine[i]
    before = shifted(after(tail, mine[TAIL]), "tm", 1)
    steps = len(bits_of(lax.axis_size("group")))
    for step in range(steps):
        if step == steps - 1:
            reduced = call(
                reduced_kernel,
                "reduced",
                [after(meta, *mine), before, hidden] + down,
                sds((half, cells, width)),
                [full] + [scratch(half * cells, width)] * 3,
            )
            earlier = reduced
        grad_time = mine_time.astype(F32) + after(group_exchange(mine_time, step, "grad_time"), earlier).astype(F32)
        if step < steps - 1:
            mine_time = grad_time.astype(BF16)
            earlier = mine_time
        else:
            earlier = grad_time
        sums = []
        for i in range(PARTS):
            other = after(group_exchange(mine[i], step, f"grad_down{i}"), earlier)
            sums.append(mine[i].astype(F32) + other.astype(F32))
            if step < steps - 1:
                mine[i] = sums[i].astype(BF16)
                earlier = mine[i]
    grad_down = jnp.concatenate(sums, axis=1)
    return reduced[None], grad_clips[None], grad_time, grad_down


def solution(mesh):
    in_specs = (
        P("group", "tm", None, None),
        P("group", None),
        P(None, "tm", None),
        P(None, "tm", None),
        P("group", "tm", None, None),
    )
    out_specs = (
        P("group", "tm", None, None),
        P("group", "tm", None, None),
        P(None, "tm", None),
        P(None, "tm", None),
    )
    return jax.shard_map(shards, mesh=mesh, in_specs=in_specs, out_specs=out_specs, check_vma=False)
```
